32 devices in a mesh: seq: 8 (over y, x, core), head: 4 (over z).
Axes of the slice: x: 2, y: 2, z: 4, core: 2. Of those that a mesh axis runs over, the one named last changes fastest.
Arguments:
- queries: bfloat16 [16, 2048, 128], P('head', 'seq'), may hold values from -9 to 9
- key_vectors: bfloat16 [16, 2048, 128], P('head', 'seq'), may hold values from -9 to 9
- value_vectors: bfloat16 [16, 2048, 128], P('head', 'seq'), may hold values from -16 to 16
- block_perm: int32 [16, 4], P('head'), may hold values from 0 to 3, each once within a row
- out_weight: bfloat16 [16, 128, 2048], P('head'), may hold values from -0.125 to 0.125
- out_cotangent: bfloat16 [2048, 2048], P('seq', 'head'), may hold values from -6 to 6
Outputs:
- projected: bfloat16 [2048, 2048], P('seq', 'head')
- gradient_of_queries: bfloat16 [16, 2048, 128], P('head', 'seq')
- key_grad: bfloat16 [16, 2048, 128], P('head', 'seq')
- value_grad: bfloat16 [16, 2048, 128], P('head', 'seq')
The draws below stay inside these ranges and needn't reach their ends.
Inputs may be any that keep to these rules, and one draw needn't show every extreme that they name: Each row of block_perm names every block of 0 to 3 once.
All inputs are finite; a program needn't handle non-finite values.
Results may differ from the reference program's by a relative error of at most 0.029.
Values may be sent and summed in bfloat16 or wider, within the bound.
No kernel may reach another device: no remote copies, remote signals or barrier semaphores. Data moves between devices by JAX's collectives and lax.ppermute only.
A program may use at most 64 MiB of HBM per device.

```python
import math
from functools import partial
import jax
import jax.numpy as jnp
from jax import lax

HD = 128
HEADS = 16
DOUT = 2048
BLOCK = 512
TOK_DEV = 256
TOKENS = 2048
NBLK = 4


def paired_rows(key):
    base = jax.random.fold_in(key, 7)
    first_key, second_key = jax.random.split(base, 2)
    shape = (HEADS, TOKENS, HD)
    query_part = jnp.clip(1.2 * jax.random.normal(first_key, shape, jnp.float32), -5.0, 5.0)
    key_part = jnp.clip(1.2 * jax.random.normal(second_key, shape, jnp.float32), -5.0, 5.0)
    return (query_part, key_part)


def draw_queries(key, part):
    return paired_rows(key)[0].astype(jnp.bfloat16)


def draw_key_vectors(key, part):
    return paired_rows(key)[1].astype(jnp.bfloat16)


def levels(stream_key, dims, pieces, smallest, top_value):
    level, own = 1.0, jax.random.fold_in(stream_key, 6)
    for axis_at, shards_of in pieces:
        steps = jnp.exp(jax.random.uniform(jax.random.fold_in(own, axis_at), (shards_of,), jnp.float32, smallest / len(pieces), top_value / len(pieces)))
        level = level * jnp.repeat(steps, dims[axis_at] // shards_of).reshape([-1 if axis == axis_at else 1 for axis in range(len(dims))])
    return level


def scatter_about(key, extent, deviation, most, pieces=(), held_as=jnp.bfloat16):
    loudness = levels(key, extent, pieces, -0.22, 0.18) if pieces else 1.0
    result = jax.random.normal(key, extent, jnp.float32) * deviation * loudness
    return jnp.minimum(jnp.maximum(result, -most), most).astype(held_as)


def setup_inputs(seed: int = 0) -> dict:
    splits = jax.random.split(jax.random.key(seed), 7)
    queries = draw_queries(jax.random.fold_in(splits[6], 71), 0)
    key_vectors = draw_key_vectors(jax.random.fold_in(splits[6], 71), 0)
    value_vectors = scatter_about(splits[2], (HEADS, TOKENS, HD), 4.0, 16.0, ((0, 4), (1, 8)))
    block_perm = jax.vmap(lambda own: jax.random.permutation(own, NBLK))(jax.random.split(splits[3], HEADS)).reshape((HEADS, NBLK)).astype(jnp.int32)
    out_weight = scatter_about(splits[4], (HEADS, HD, DOUT), (HEADS * HD) ** -0.5, 0.125, ((0, 4),))
    out_cotangent = scatter_about(splits[5], (TOKENS, DOUT), 1.0, 6.0, ((0, 8), (1, 4)))
    return {"queries": queries, "key_vectors": key_vectors, "value_vectors": value_vectors, "block_perm": block_perm, "out_weight": out_weight, "out_cotangent": out_cotangent}


def to_low(values):
    return lax.optimization_barrier(values.astype(jnp.bfloat16)).astype(jnp.float32)

def split_terms(half_terms, order, nblocks):
    local = half_terms[:, :, :BLOCK].reshape(nblocks, 2, 2, TOK_DEV, HD)
    own = jnp.stack([local[:, 0, 0], local[:, 1, 1]], axis=1).reshape(nblocks, BLOCK, HD)
    pair = jnp.stack([local[:, 1, 0], local[:, 0, 1]], axis=1).reshape(nblocks, BLOCK, HD)
    partner = to_low(half_terms[:, 0, BLOCK:]) + to_low(half_terms[:, 1, BLOCK:])
    zeros_blocks = jnp.zeros((nblocks, BLOCK, HD), jnp.float32)
    moved = zeros_blocks.at[order].add(partner)
    remote = to_low(to_low(pair) + moved)
    return (own + remote).astype(jnp.bfloat16).reshape(TOKENS, HD)

def head_pass(cotangent, carry, inputs):
    query_rows, key_rows, value_rows, order, weight_rows = inputs
    nblocks = TOKENS // BLOCK
    scale_factor = 1.0 / math.sqrt(HD)
    query_by_block = query_rows.reshape(nblocks, BLOCK, HD).astype(jnp.float32)
    blocked_k = key_rows.reshape(nblocks, BLOCK, HD).astype(jnp.float32)
    blocked_v = value_rows.reshape(nblocks, BLOCK, HD).astype(jnp.float32)
    joined_keys = jnp.concatenate([blocked_k, blocked_k[order]], axis=1)
    joined_values = jnp.concatenate([blocked_v, blocked_v[order]], axis=1)
    logit_scores = jnp.einsum('nsx,nox->nso', query_by_block, joined_keys) * scale_factor
    row_max = lax.optimization_barrier(jnp.max(logit_scores, axis=-1, keepdims=True))
    weights = jnp.exp(logit_scores - row_max)
    probabilities = weights / lax.optimization_barrier(jnp.sum(weights, axis=-1, keepdims=True))
    reduced_probabilities = lax.optimization_barrier(probabilities.astype(jnp.bfloat16)).astype(jnp.float32)
    attention_result = jnp.einsum('osa,oam->osm', reduced_probabilities, joined_values).astype(jnp.bfloat16)
    attention_result = lax.optimization_barrier(attention_result)
    flat_att = attention_result.reshape(TOKENS, HD)
    carry = carry + jnp.dot(flat_att, weight_rows, preferred_element_type=jnp.float32)
    grad_att = jnp.dot(cotangent, weight_rows.T, preferred_element_type=jnp.float32).astype(jnp.bfloat16)
    grad_att = lax.optimization_barrier(grad_att)
    gradient_by_block = grad_att.reshape(nblocks, BLOCK, HD).astype(jnp.float32)
    row_delta = lax.optimization_barrier(jnp.sum(gradient_by_block * attention_result.astype(jnp.float32), axis=-1, keepdims=True))
    probability_gradient = jnp.einsum('nsx,nox->nso', gradient_by_block, joined_values)
    score_gradient = (probabilities * (probability_gradient - row_delta) * scale_factor).astype(jnp.bfloat16)
    score_gradient = lax.optimization_barrier(score_gradient).astype(jnp.float32)
    gradient_of_queries = jnp.einsum('osa,oam->osm', score_gradient, joined_keys).astype(jnp.bfloat16)
    halves_s = score_gradient.reshape(nblocks, 2, TOK_DEV, 2 * BLOCK)
    halves_p = reduced_probabilities.reshape(nblocks, 2, TOK_DEV, 2 * BLOCK)
    halves_q = query_by_block.reshape(nblocks, 2, TOK_DEV, HD)
    halves_g = gradient_by_block.reshape(nblocks, 2, TOK_DEV, HD)
    key_half = jnp.einsum('burk,burd->bukd', halves_s, halves_q)
    value_half = jnp.einsum('burk,burd->bukd', halves_p, halves_g)
    outputs = (gradient_of_queries.reshape(TOKENS, HD), split_terms(key_half, order, nblocks), split_terms(value_half, order, nblocks))
    return (carry, outputs)

def reference(queries, key_vectors, value_vectors, block_perm, out_weight, out_cotangent):
    initial = jnp.zeros((TOKENS, DOUT), jnp.float32)
    summed, grads = lax.scan(partial(head_pass, out_cotangent), initial, (queries, key_vectors, value_vectors, block_perm, out_weight))
    return (summed.astype(jnp.bfloat16), grads[0], grads[1], grads[2])
```

```python
import functools
import math

import jax
import jax.numpy as jnp
from jax import lax
from jax.experimental import pallas as pl
from jax.experimental.pallas import tpu as pltpu
from jax.sharding import PartitionSpec as P

F32 = jnp.float32
LOW = jnp.bfloat16
NT = (((1,), (1,)), ((), ()))
NN = (((1,), (0,)), ((), ()))
TN = (((0,), (0,)), ((), ()))


def dot(a, b, dims=NN):
    return lax.dot_general(a, b, dims, preferred_element_type=F32)


def chip_index():
    return lax.axis_index("seq") // 2


def call(body, outs, *args, flops=0, moved=0, scratch=(), smem=()):
    vmem = pl.BlockSpec(memory_space=pltpu.VMEM)
    scalar = pl.BlockSpec(memory_space=pltpu.SMEM)
    return pl.pallas_call(
        body,
        out_shape=outs,
        in_specs=[scalar if i in smem else vmem for i in range(len(args))],
        out_specs=jax.tree.map(lambda _: vmem, outs),
        scratch_shapes=list(scratch),
        cost_estimate=pl.CostEstimate(flops=flops, bytes_accessed=moved, transcendentals=0),
        compiler_params=pltpu.CompilerParams(vmem_limit_bytes=48 * 1024 * 1024),
    )(*args)


def attend_body(chips, rows, scale, perm, *refs):
    pieces, siblings = refs[:chips], refs[chips : 2 * chips]
    attended, probs, keys_values, queries = refs[2 * chips :]
    chip = chip_index()
    for d in range(chips):
        for kind in range(2):
            keys_values[d, kind, :rows] = pieces[d][kind]
            keys_values[d, kind, rows:] = siblings[d][kind]
        queries[d] = pieces[d][2]
    for d in range(chips):
        p = perm[chip, chip ^ d] ^ chip
        query = pieces[d][2]
        local = dot(query, keys_values[d, 0], NT)
        remote = dot(query, keys_values[p, 0], NT)
        top = jnp.maximum(
            jnp.max(local, axis=1, keepdims=True), jnp.max(remote, axis=1, keepdims=True)
        )
        factor = scale * math.log2(math.e)
        local = jnp.exp2((local - top) * factor)
        remote = jnp.exp2((remote - top) * factor)
        total = jnp.sum(local, axis=1, keepdims=True) + jnp.sum(remote, axis=1, keepdims=True)
        share = 1.0 / total
        local = (local * share).astype(LOW)
        remote = (remote * share).astype(LOW)
        probs[d, :, : 2 * rows] = local
        probs[d, :, 2 * rows :] = remote
        result = dot(local, keys_values[d, 1]) + dot(remote, keys_values[p, 1])
        attended[d] = result.astype(LOW)


def backward_body(chips, rows, scale, perm, *refs):
    arrived = refs[:chips]
    attended, probs, keys_values, queries = refs[chips : chips + 4]
    query_grad, own_part, sibling_part, score_grad, grads = refs[chips + 4 :]
    chip = chip_index()
    for d in range(chips):
        p = perm[chip, chip ^ d] ^ chip
        grad = arrived[d][...]
        grads[d] = grad
        delta = jnp.sum(grad.astype(F32) * attended[d].astype(F32), axis=1, keepdims=True)
        total = None
        for part, source in ((0, d), (1, p)):
            lanes = slice(2 * rows * part, 2 * rows * (part + 1))
            prob_grad = dot(grad, keys_values[source, 1], NT)
            weight = probs[d, :, lanes].astype(F32)
            change = (weight * (prob_grad - delta) * scale).astype(LOW)
            score_grad[part, d] = change
            term = dot(change, keys_values[source, 0])
            total = term if total is None else total + term
        query_grad[d] = total.astype(LOW)
    for d in range(chips):
        asker = jnp.int32(0)
        for i in range(chips):
            asker = jnp.where(perm[chip, i] == chip ^ d, i, asker)
        asker = asker ^ chip
        for half, out in ((0, own_part), (1, sibling_part)):
            near = slice(half * rows, (half + 1) * rows)
            far = slice((half + 2) * rows, (half + 3) * rows)
            key_part = dot(score_grad[0, d, :, near], queries[d], TN)
            key_part += dot(score_grad[1, asker, :, near], queries[asker], TN)
            value_part = dot(probs[d, :, near], grads[d], TN)
            value_part += dot(probs[asker, :, far], grads[asker], TN)
            out[d, 0] = key_part.astype(out.dtype)
            out[d, 1] = value_part.astype(out.dtype)


def project_body(chips, weight, *refs):
    attended, out, joined = refs[:chips], refs[chips], refs[chips + 1]
    chip = chip_index()
    width = attended[0].shape[1]
    for d in range(chips):
        lanes = pl.ds(pl.multiple_of((chip ^ d) * width, width), width)
        joined[:, lanes] = attended[d][...]
    columns = out.shape[2]
    rows = joined[...]
    flat = weight.reshape(chips * width, weight.shape[2])
    for s in range(out.shape[0]):
        out[s] = dot(rows, flat[:, s * columns : (s + 1) * columns]).astype(out.dtype)


def grad_body(chips, weight, cotangent, out):
    chip = chip_index()
    width = out.shape[2]
    columns = cotangent.shape[2]
    flat = weight.reshape(chips * width, weight.shape[2])
    total = None
    for s in range(cotangent.shape[0]):
        term = dot(cotangent[s], flat[:, s * columns : (s + 1) * columns], NT)
        total = term if total is None else total + term
    for h in range(chips):
        out[h ^ chip] = total[:, h * width : (h + 1) * width].astype(out.dtype)


def merge_body(chips, query_grad, own_part, arrived, *outs):
    for d in range(chips):
        outs[d][0] = query_grad[d]
        for kind in range(2):
            both = own_part[d, kind] + arrived[d, kind].astype(F32)
            outs[d][1 + kind] = both.astype(LOW)


def place_body(chips, *refs):
    pieces, outs = refs[:chips], refs[chips:]
    chip = chip_index()
    for d in range(chips):
        for kind in range(3):
            outs[kind][chip ^ d] = pieces[d][kind]


def by_heads(queries, key_vectors, value_vectors, block_perm, out_weight, out_cotangent):
    devices = lax.axis_size("seq")
    chips = devices // 2
    groups = lax.axis_size("head")
    heads, rows, width = queries.shape
    features = out_weight.shape[2]
    columns = out_cotangent.shape[1]
    scale = 1.0 / math.sqrt(width)
    chip = chip_index()
    shape = jax.ShapeDtypeStruct

    def to_chip(array, d):
        return lax.ppermute(array, "seq", [(i, i ^ (2 * d)) for i in range(devices)])

    def to_sibling(array):
        return lax.ppermute(array, "seq", [(i, i ^ 1) for i in range(devices)])

    def exchange(pieces):
        return [pieces[0]] + [to_chip(pieces[d], d) for d in range(1, chips)]

    def head_piece(d):
        h = chip ^ d
        return jnp.stack(
            [
                lax.dynamic_index_in_dim(a, h, 0, keepdims=False)
                for a in (key_vectors, value_vectors, queries)
            ]
        )

    gathered = lax.all_gather(out_cotangent, "head", axis=0, tiled=False)
    pieces = exchange([head_piece(d) for d in range(chips)])
    siblings = [to_sibling(piece[:2]) for piece in pieces]
    tile = rows * width
    scores = chips * rows * 4 * rows
    attended, probs, keys_values, query_rows = call(
        functools.partial(attend_body, chips, rows, scale),
        (
            shape((chips, rows, width), LOW),
            shape((chips, rows, 4 * rows), LOW),
            shape((chips, 2, 2 * rows, width), LOW),
            shape((chips, rows, width), LOW),
        ),
        block_perm,
        *pieces,
        *siblings,
        flops=4 * scores * width,
        moved=2 * (scores + 14 * chips * tile),
        smem=(0,),
    )
    weight_bytes = 2 * heads * width * features
    grad_att = call(
        functools.partial(grad_body, chips),
        shape((chips, rows, width), LOW),
        out_weight,
        gathered,
        flops=2 * rows * heads * width * features,
        moved=weight_bytes + 2 * rows * features + 2 * chips * tile,
    )
    grads = exchange([grad_att[d] for d in range(chips)])
    own_attended = exchange([attended[d] for d in range(chips)])
    partial_out = call(
        functools.partial(project_body, chips),
        shape((groups, rows, columns), LOW),
        out_weight,
        *own_attended,
        flops=2 * rows * heads * width * features,
        moved=weight_bytes + 2 * rows * features + 2 * chips * tile,
        scratch=[pltpu.VMEM((rows, heads * width), LOW)],
    )
    projected = lax.psum_scatter(partial_out, "head", scatter_dimension=0, tiled=False)
    query_grad, own_part, sibling_part = call(
        functools.partial(backward_body, chips, rows, scale),
        (
            shape((chips, rows, width), LOW),
            shape((chips, 2, rows, width), F32),
            shape((chips, 2, rows, width), LOW),
        ),
        block_perm,
        *grads,
        attended,
        probs,
        keys_values,
        query_rows,
        flops=8 * scores * width,
        moved=2 * (scores + 20 * chips * tile),
        scratch=[
            pltpu.VMEM((2, chips, rows, 2 * rows), LOW),
            pltpu.VMEM((chips, rows, width), LOW),
        ],
        smem=(0,),
    )
    returned = exchange(
        call(
            functools.partial(merge_body, chips),
            tuple(shape((3, rows, width), LOW) for _ in range(chips)),
            query_grad,
            own_part,
            to_sibling(sibling_part),
            moved=2 * 14 * chips * tile,
        )
    )
    gradients = call(
        functools.partial(place_body, chips),
        tuple(shape((heads, rows, width), LOW) for _ in range(3)),
        *returned,
        moved=2 * 6 * chips * tile,
    )
    return (projected, *gradients)


def partner(shard, axis, bit):
    return lax.ppermute(shard, axis, [(i, i ^ 1 << bit) for i in range(lax.axis_size(axis))])


def by_routing(queries, key_vectors, value_vectors, block_perm, out_weight, out_cotangent):
    devices = lax.axis_size("seq")
    position = lax.axis_index("seq")
    parity = position % 2
    group_heads, tok_rows, head_width = queries.shape
    portion = tok_rows * head_width // devices
    score_scale = 1.0 / math.sqrt(head_width)
    owners = jnp.repeat(block_perm, 2, axis=1)
    indices = lax.iota(jnp.int32, devices)
    sources = [2 * owners, 2 * owners + 1]
    source_table = jnp.stack(sources, axis=1)
    slot_count = source_table.shape[1]
    select = (source_table[..., None] == indices).astype(jnp.bfloat16)
    stacked = jnp.stack([key_vectors, value_vectors])
    spread = lax.all_to_all(
        stacked.reshape(2, group_heads, devices, portion),
        "seq",
        split_axis=2,
        concat_axis=2,
        tiled=True,
    )
    picked = jnp.einsum(
        "hsij,chjl->chsil", select, spread, preferred_element_type=jnp.float32
    ).astype(jnp.bfloat16)
    routed = lax.all_to_all(picked, "seq", split_axis=3, concat_axis=3, tiled=True)
    routed = routed.reshape(2, group_heads, slot_count, tok_rows, head_width)
    partner_kv = routed.reshape(2, group_heads, 2 * tok_rows, head_width)
    pair_other = partner(stacked, "seq", 0)
    local_kv = jnp.where(
        parity == 0,
        jnp.concatenate([stacked, pair_other], 2),
        jnp.concatenate([pair_other, stacked], 2),
    )
    combined = jnp.concatenate([local_kv, partner_kv], 2)
    key_all = combined[0]
    value_all = combined[1]
    logit_scores = (
        jnp.einsum("htd,hkd->htk", queries, key_all, preferred_element_type=jnp.float32)
        * score_scale
    )
    row_max = jnp.max(logit_scores, axis=-1, keepdims=True)
    weights = jnp.exp(logit_scores - row_max)
    probabilities = weights / jnp.sum(weights, axis=-1, keepdims=True)
    reduced_probabilities = probabilities.astype(jnp.bfloat16)
    attention_result = jnp.einsum(
        "htk,hkd->htd", reduced_probabilities, value_all, preferred_element_type=jnp.float32
    ).astype(jnp.bfloat16)
    partial_out = jnp.einsum(
        "htd,hde->te", attention_result, out_weight, preferred_element_type=jnp.float32
    )
    summed = lax.psum(partial_out.astype(jnp.bfloat16), "head").astype(jnp.float32)
    columns = summed.shape[1] // lax.axis_size("head")
    result = lax.dynamic_slice_in_dim(summed, lax.axis_index("head") * columns, columns, 1)
    projected = result.astype(jnp.bfloat16)
    full_grad = lax.all_gather(out_cotangent, "head", axis=1, tiled=True)
    grad_att = jnp.einsum(
        "te,hde->htd", full_grad, out_weight, preferred_element_type=jnp.float32
    ).astype(jnp.bfloat16)
    row_delta = jnp.sum(
        grad_att.astype(jnp.float32) * attention_result.astype(jnp.float32), axis=-1, keepdims=True
    )
    probability_gradient = jnp.einsum(
        "htd,hkd->htk", grad_att, value_all, preferred_element_type=jnp.float32
    )
    score_gradient = (probabilities * (probability_gradient - row_delta) * score_scale).astype(
        jnp.bfloat16
    )
    gradient_of_queries = jnp.einsum(
        "htk,hkd->htd", score_gradient, key_all, preferred_element_type=jnp.float32
    ).astype(jnp.bfloat16)
    key_part = jnp.einsum(
        "htk,htd->hkd", score_gradient, queries, preferred_element_type=jnp.float32
    )
    value_part = jnp.einsum(
        "htk,htd->hkd", reduced_probabilities, grad_att, preferred_element_type=jnp.float32
    )
    gradients = jnp.stack([key_part, value_part])
    block_rows = 2 * tok_rows
    local_grad = gradients[:, :, :block_rows].reshape(2, group_heads, 2, tok_rows, head_width)
    own_grad = jnp.where(parity == 0, local_grad[:, :, 0], local_grad[:, :, 1])
    other_grad = jnp.where(parity == 0, local_grad[:, :, 1], local_grad[:, :, 0]).astype(
        jnp.bfloat16
    )
    partner_grad = gradients[:, :, block_rows:].reshape(2, group_heads, 2, tok_rows, head_width)
    partner_grad = partner_grad.astype(jnp.bfloat16)
    returned = lax.all_to_all(
        partner_grad.reshape(2, group_heads, slot_count, devices, portion),
        "seq",
        split_axis=3,
        concat_axis=3,
        tiled=True,
    )
    summed_back = jnp.einsum(
        "hsij,chsil->chjl", select, returned, preferred_element_type=jnp.float32
    ).astype(jnp.bfloat16)
    arrived = lax.all_to_all(summed_back, "seq", split_axis=2, concat_axis=2, tiled=True)
    arrived = arrived.reshape(2, group_heads, tok_rows, head_width).astype(jnp.float32)
    pair_back = partner(other_grad, "seq", 0).astype(jnp.float32)
    total_grad = own_grad + arrived + pair_back
    key_grad = total_grad[0].astype(jnp.bfloat16)
    value_grad = total_grad[1].astype(jnp.bfloat16)
    return (projected, gradient_of_queries, key_grad, value_grad)


def per_device(*arrays):
    chips = lax.axis_size("seq") // 2
    square = chips == arrays[0].shape[0] and chips & (chips - 1) == 0
    return (by_heads if square else by_routing)(*arrays)


def solution(mesh):
    return jax.shard_map(
        per_device,
        mesh=mesh,
        in_specs=(
            P("head", "seq", None),
            P("head", "seq", None),
            P("head", "seq", None),
            P("head", None),
            P("head", None, None),
            P("seq", "head"),
        ),
        out_specs=(
            P("seq", "head"),
            P("head", "seq", None),
            P("head", "seq", None),
            P("head", "seq", None),
        ),
        check_vma=False,
    )
```

```python
import functools
import math

import jax
import jax.numpy as jnp
from jax import lax
from jax.experimental import pallas as pl
from jax.experimental.pallas import tpu as pltpu
from jax.sharding import PartitionSpec as P

F32 = jnp.float32
LOW = jnp.bfloat16
NT = (((1,), (1,)), ((), ()))
NN = (((1,), (0,)), ((), ()))
TN = (((0,), (0,)), ((), ()))


def dot(a, b, dims=NN):
    return lax.dot_general(a, b, dims, preferred_element_type=F32)


def chip_index():
    return lax.axis_index("seq") // 2


def call(body, outs, *args, flops=0, moved=0, scratch=(), smem=()):
    vmem = pl.BlockSpec(memory_space=pltpu.VMEM)
    scalar = pl.BlockSpec(memory_space=pltpu.SMEM)
    return pl.pallas_call(
        body,
        out_shape=outs,
        in_specs=[scalar if i in smem else vmem for i in range(len(args))],
        out_specs=jax.tree.map(lambda _: vmem, outs),
        scratch_shapes=list(scratch),
        cost_estimate=pl.CostEstimate(flops=flops, bytes_accessed=moved, transcendentals=0),
        compiler_params=pltpu.CompilerParams(vmem_limit_bytes=48 * 1024 * 1024),
    )(*args)


def attend_body(chips, rows, scale, perm, *refs):
    pieces, siblings = refs[:chips], refs[chips : 2 * chips]
    attended, probs, keys_values, queries = refs[2 * chips :]
    chip = chip_index()
    for d in range(chips):
        for kind in range(2):
            keys_values[d, kind, :rows] = pieces[d][kind]
            keys_values[d, kind, rows:] = siblings[d][kind]
        queries[d] = pieces[d][2]
    for d in range(chips):
        p = perm[chip, chip ^ d] ^ chip
        query = pieces[d][2]
        local = dot(query, keys_values[d, 0], NT)
        remote = dot(query, keys_values[p, 0], NT)
        top = jnp.maximum(
            jnp.max(local, axis=1, keepdims=True), jnp.max(remote, axis=1, keepdims=True)
        )
        factor = scale * math.log2(math.e)
        local = jnp.exp2((local - top) * factor)
        remote = jnp.exp2((remote - top) * factor)
        total = jnp.sum(local, axis=1, keepdims=True) + jnp.sum(remote, axis=1, keepdims=True)
        share = 1.0 / total
        local = (local * share).astype(LOW)
        remote = (remote * share).astype(LOW)
        probs[d, :, : 2 * rows] = local
        probs[d, :, 2 * rows :] = remote
        result = dot(local, keys_values[d, 1]) + dot(remote, keys_values[p, 1])
        attended[d] = result.astype(LOW)


def backward_body(chips, rows, scale, perm, *refs):
    arrived = refs[:chips]
    attended, probs, keys_values, queries = refs[chips : chips + 4]
    query_grad, own_part, sibling_part, score_grad, grads = refs[chips + 4 :]
    chip = chip_index()
    for d in range(chips):
        p = perm[chip, chip ^ d] ^ chip
        grad = arrived[d][...]
        grads[d] = grad
        delta = jnp.sum(grad.astype(F32) * attended[d].astype(F32), axis=1, keepdims=True)
        total = None
        for part, source in ((0, d), (1, p)):
            lanes = slice(2 * rows * part, 2 * rows * (part + 1))
            prob_grad = dot(grad, keys_values[source, 1], NT)
            weight = probs[d, :, lanes].astype(F32)
            change = (weight * (prob_grad - delta) * scale).astype(LOW)
            score_grad[part, d] = change
            term = dot(change, keys_values[source, 0])
            total = term if total is None else total + term
        query_grad[d] = total.astype(LOW)
    for d in range(chips):
        asker = jnp.int32(0)
        for i in range(chips):
            asker = jnp.where(perm[chip, i] == chip ^ d, i, asker)
        asker = asker ^ chip
        for half, out in ((0, own_part), (1, sibling_part)):
            near = slice(half * rows, (half + 1) * rows)
            far = slice((half + 2) * rows, (half + 3) * rows)
            key_part = dot(score_grad[0, d, :, near], queries[d], TN)
            key_part += dot(score_grad[1, asker, :, near], queries[asker], TN)
            value_part = dot(probs[d, :, near], grads[d], TN)
            value_part += dot(probs[asker, :, far], grads[asker], TN)
            out[d, 0] = key_part.astype(out.dtype)
            out[d, 1] = value_part.astype(out.dtype)


def project_body(chips, groups, weight, *refs):
    attended, outs, joined = refs[:chips], refs[chips : chips + groups], refs[chips + groups]
    chip = chip_index()
    level = lax.axis_index("head")
    width = attended[0].shape[1]
    for d in range(chips):
        lanes = pl.ds(pl.multiple_of((chip ^ d) * width, width), width)
        joined[:, lanes] = attended[d][...]
    rows = joined[...]
    for j in range(groups):
        columns = outs[j].shape[1]
        lanes = pl.ds(pl.multiple_of((level ^ j) * columns, columns), columns)
        term = weight[:, :, lanes].reshape(chips * width, columns)
        outs[j][...] = dot(rows, term).astype(LOW)


def grad_body(chips, groups, weight, *refs):
    slices, out = refs[:-1], refs[-1]
    chip = chip_index()
    level = lax.axis_index("head")
    inner = (level > 0) & (level < groups - 1)
    width = out.shape[2]
    total = None
    for j in range(groups):
        if j < 2:
            block = slices[j][...]
        else:
            block = jnp.where(inner, slices[2 * j - 2][...], slices[2 * j - 1][...])
        columns = block.shape[1]
        lanes = pl.ds(pl.multiple_of((level ^ j) * columns, columns), columns)
        term = dot(block, weight[:, :, lanes].reshape(chips * width, columns), NT)
        total = term if total is None else total + term
    for h in range(chips):
        out[h ^ chip] = total[:, h * width : (h + 1) * width].astype(LOW)


def merge_body(chips, query_grad, own_part, arrived, *outs):
    for d in range(chips):
        outs[d][0] = query_grad[d]
        for kind in range(2):
            both = own_part[d, kind] + arrived[d, kind].astype(F32)
            outs[d][1 + kind] = both.astype(LOW)


def place_body(chips, *refs):
    pieces, outs = refs[:chips], refs[chips:]
    chip = chip_index()
    for d in range(chips):
        for kind in range(3):
            outs[kind][chip ^ d] = pieces[d][kind]


def by_heads(queries, key_vectors, value_vectors, block_perm, out_weight, out_cotangent):
    devices = lax.axis_size("seq")
    chips = devices // 2
    groups = lax.axis_size("head")
    heads, rows, width = queries.shape
    features = out_weight.shape[2]
    columns = out_cotangent.shape[1]
    scale = 1.0 / math.sqrt(width)
    chip = chip_index()
    shape = jax.ShapeDtypeStruct

    def to_chip(array, d):
        return lax.ppermute(array, "seq", [(i, i ^ (2 * d)) for i in range(devices)])

    def to_sibling(array):
        return lax.ppermute(array, "seq", [(i, i ^ 1) for i in range(devices)])

    def exchange(pieces):
        return [pieces[0]] + [to_chip(pieces[d], d) for d in range(1, chips)]

    def head_piece(d):
        h = chip ^ d
        return jnp.stack(
            [
                lax.dynamic_index_in_dim(a, h, 0, keepdims=False)
                for a in (key_vectors, value_vectors, queries)
            ]
        )

    def along(array, pairs):
        return lax.ppermute(array, "head", pairs)

    skip_in = along(out_cotangent, [(0, 2), (3, 1)])
    pair_in = along(out_cotangent, [(0, 1), (1, 0), (2, 3), (3, 2)])
    middle_in = along(out_cotangent, [(1, 2), (2, 1)])
    pieces = exchange([head_piece(d) for d in range(chips)])
    siblings = [to_sibling(piece[:2]) for piece in pieces]
    tile = rows * width
    scores = chips * rows * 4 * rows
    attended, probs, keys_values, query_rows = call(
        functools.partial(attend_body, chips, rows, scale),
        (
            shape((chips, rows, width), LOW),
            shape((chips, rows, 4 * rows), LOW),
            shape((chips, 2, 2 * rows, width), LOW),
            shape((chips, rows, width), LOW),
        ),
        block_perm,
        *pieces,
        *siblings,
        flops=4 * scores * width,
        moved=2 * (scores + 14 * chips * tile),
        smem=(0,),
    )
    weight_bytes = 2 * heads * width * features
    far_in = along(skip_in, [(2, 3), (1, 0)])
    near_in = along(middle_in, [(2, 3), (1, 0)])
    grad_att = call(
        functools.partial(grad_body, chips, groups),
        shape((chips, rows, width), LOW),
        out_weight,
        out_cotangent,
        pair_in,
        skip_in,
        near_in,
        middle_in,
        far_in,
        flops=2 * rows * heads * width * features,
        moved=weight_bytes + 2 * rows * features + 2 * chips * tile,
    )
    grads = exchange([grad_att[d] for d in range(chips)])
    own_attended = exchange([attended[d] for d in range(chips)])
    parts = call(
        functools.partial(project_body, chips, groups),
        tuple(shape((rows, columns), LOW) for _ in range(groups)),
        out_weight,
        *own_attended,
        flops=2 * rows * heads * width * features,
        moved=weight_bytes + 2 * rows * features + 2 * chips * tile,
        scratch=[pltpu.VMEM((rows, heads * width), LOW)],
    )

    def plus(a, b):
        return (a.astype(F32) + b.astype(F32)).astype(LOW)

    end_far = along(parts[3], [(3, 2), (0, 1)])
    end_near = along(parts[2], [(3, 2), (0, 1)])
    pair_out = along(parts[1], [(0, 1), (1, 0), (2, 3), (3, 2)])
    skip_out = along(plus(parts[2], end_far), [(2, 0), (1, 3)])
    middle_out = along(plus(parts[3], end_near), [(2, 1), (1, 2)])
    query_grad, own_part, sibling_part = call(
        functools.partial(backward_body, chips, rows, scale),
        (
            shape((chips, rows, width), LOW),
            shape((chips, 2, rows, width), F32),
            shape((chips, 2, rows, width), LOW),
        ),
        block_perm,
        *grads,
        attended,
        probs,
        keys_values,
        query_rows,
        flops=8 * scores * width,
        moved=2 * (scores + 20 * chips * tile),
        scratch=[
            pltpu.VMEM((2, chips, rows, 2 * rows), LOW),
            pltpu.VMEM((chips, rows, width), LOW),
        ],
        smem=(0,),
    )
    returned = exchange(
        call(
            functools.partial(merge_body, chips),
            tuple(shape((3, rows, width), LOW) for _ in range(chips)),
            query_grad,
            own_part,
            to_sibling(sibling_part),
            moved=2 * 14 * chips * tile,
        )
    )
    gradients = call(
        functools.partial(place_body, chips),
        tuple(shape((heads, rows, width), LOW) for _ in range(3)),
        *returned,
        moved=2 * 6 * chips * tile,
    )
    level = lax.axis_index("head")
    inner = (level > 0) & (level < groups - 1)
    passed = jnp.where(inner, middle_out, skip_out)
    projected = parts[0].astype(F32) + pair_out.astype(F32) + passed.astype(F32)
    return (projected.astype(LOW), *gradients)


def partner(shard, axis, bit):
    return lax.ppermute(shard, axis, [(i, i ^ 1 << bit) for i in range(lax.axis_size(axis))])


def by_routing(queries, key_vectors, value_vectors, block_perm, out_weight, out_cotangent):
    devices = lax.axis_size("seq")
    position = lax.axis_index("seq")
    parity = position % 2
    group_heads, tok_rows, head_width = queries.shape
    portion = tok_rows * head_width // devices
    score_scale = 1.0 / math.sqrt(head_width)
    owners = jnp.repeat(block_perm, 2, axis=1)
    indices = lax.iota(jnp.int32, devices)
    sources = [2 * owners, 2 * owners + 1]
    source_table = jnp.stack(sources, axis=1)
    slot_count = source_table.shape[1]
    select = (source_table[..., None] == indices).astype(jnp.bfloat16)
    stacked = jnp.stack([key_vectors, value_vectors])
    spread = lax.all_to_all(
        stacked.reshape(2, group_heads, devices, portion),
        "seq",
        split_axis=2,
        concat_axis=2,
        tiled=True,
    )
    picked = jnp.einsum(
        "hsij,chjl->chsil", select, spread, preferred_element_type=jnp.float32
    ).astype(jnp.bfloat16)
    routed = lax.all_to_all(picked, "seq", split_axis=3, concat_axis=3, tiled=True)
    routed = routed.reshape(2, group_heads, slot_count, tok_rows, head_width)
    partner_kv = routed.reshape(2, group_heads, 2 * tok_rows, head_width)
    pair_other = partner(stacked, "seq", 0)
    local_kv = jnp.where(
        parity == 0,
        jnp.concatenate([stacked, pair_other], 2),
        jnp.concatenate([pair_other, stacked], 2),
    )
    combined = jnp.concatenate([local_kv, partner_kv], 2)
    key_all = combined[0]
    value_all = combined[1]
    logit_scores = (
        jnp.einsum("htd,hkd->htk", queries, key_all, preferred_element_type=jnp.float32)
        * score_scale
    )
    row_max = jnp.max(logit_scores, axis=-1, keepdims=True)
    weights = jnp.exp(logit_scores - row_max)
    probabilities = weights / jnp.sum(weights, axis=-1, keepdims=True)
    reduced_probabilities = probabilities.astype(jnp.bfloat16)
    attention_result = jnp.einsum(
        "htk,hkd->htd", reduced_probabilities, value_all, preferred_element_type=jnp.float32
    ).astype(jnp.bfloat16)
    partial_out = jnp.einsum(
        "htd,hde->te", attention_result, out_weight, preferred_element_type=jnp.float32
    )
    summed = lax.psum(partial_out.astype(jnp.bfloat16), "head").astype(jnp.float32)
    columns = summed.shape[1] // lax.axis_size("head")
    result = lax.dynamic_slice_in_dim(summed, lax.axis_index("head") * columns, columns, 1)
    projected = result.astype(jnp.bfloat16)
    full_grad = lax.all_gather(out_cotangent, "head", axis=1, tiled=True)
    grad_att = jnp.einsum(
        "te,hde->htd", full_grad, out_weight, preferred_element_type=jnp.float32
    ).astype(jnp.bfloat16)
    row_delta = jnp.sum(
        grad_att.astype(jnp.float32) * attention_result.astype(jnp.float32), axis=-1, keepdims=True
    )
    probability_gradient = jnp.einsum(
        "htd,hkd->htk", grad_att, value_all, preferred_element_type=jnp.float32
    )
    score_gradient = (probabilities * (probability_gradient - row_delta) * score_scale).astype(
        jnp.bfloat16
    )
    gradient_of_queries = jnp.einsum(
        "htk,hkd->htd", score_gradient, key_all, preferred_element_type=jnp.float32
    ).astype(jnp.bfloat16)
    key_part = jnp.einsum(
        "htk,htd->hkd", score_gradient, queries, preferred_element_type=jnp.float32
    )
    value_part = jnp.einsum(
        "htk,htd->hkd", reduced_probabilities, grad_att, preferred_element_type=jnp.float32
    )
    gradients = jnp.stack([key_part, value_part])
    block_rows = 2 * tok_rows
    local_grad = gradients[:, :, :block_rows].reshape(2, group_heads, 2, tok_rows, head_width)
    own_grad = jnp.where(parity == 0, local_grad[:, :, 0], local_grad[:, :, 1])
    other_grad = jnp.where(parity == 0, local_grad[:, :, 1], local_grad[:, :, 0]).astype(
        jnp.bfloat16
    )
    partner_grad = gradients[:, :, block_rows:].reshape(2, group_heads, 2, tok_rows, head_width)
    partner_grad = partner_grad.astype(jnp.bfloat16)
    returned = lax.all_to_all(
        partner_grad.reshape(2, group_heads, slot_count, devices, portion),
        "seq",
        split_axis=3,
        concat_axis=3,
        tiled=True,
    )
    summed_back = jnp.einsum(
        "hsij,chsil->chjl", select, returned, preferred_element_type=jnp.float32
    ).astype(jnp.bfloat16)
    arrived = lax.all_to_all(summed_back, "seq", split_axis=2, concat_axis=2, tiled=True)
    arrived = arrived.reshape(2, group_heads, tok_rows, head_width).astype(jnp.float32)
    pair_back = partner(other_grad, "seq", 0).astype(jnp.float32)
    total_grad = own_grad + arrived + pair_back
    key_grad = total_grad[0].astype(jnp.bfloat16)
    value_grad = total_grad[1].astype(jnp.bfloat16)
    return (projected, gradient_of_queries, key_grad, value_grad)


def per_device(*arrays):
    chips = lax.axis_size("seq") // 2
    square = chips == arrays[0].shape[0] == lax.axis_size("head") == 4
    return (by_heads if square else by_routing)(*arrays)


def solution(mesh):
    return jax.shard_map(
        per_device,
        mesh=mesh,
        in_specs=(
            P("head", "seq", None),
            P("head", "seq", None),
            P("head", "seq", None),
            P("head", None),
            P("head", None, None),
            P("seq", "head"),
        ),
        out_specs=(
            P("seq", "head"),
            P("head", "seq", None),
            P("head", "seq", None),
            P("head", "seq", None),
        ),
        check_vma=False,
    )
```

```python
import functools
import math

import jax
import jax.numpy as jnp
from jax import lax
from jax.experimental import pallas as pl
from jax.experimental.pallas import tpu as pltpu
from jax.sharding import PartitionSpec as P

F32 = jnp.float32
LOW = jnp.bfloat16
NT = (((1,), (1,)), ((), ()))
NN = (((1,), (0,)), ((), ()))
TN = (((0,), (0,)), ((), ()))


def dot(a, b, dims=NN):
    return lax.dot_general(a, b, dims, preferred_element_type=F32)


def chip_index():
    return lax.axis_index("seq") // 2


def call(body, outs, *args, flops=0, moved=0, scratch=(), smem=()):
    vmem = pl.BlockSpec(memory_space=pltpu.VMEM)
    scalar = pl.BlockSpec(memory_space=pltpu.SMEM)
    return pl.pallas_call(
        body,
        out_shape=outs,
        in_specs=[scalar if i in smem else vmem for i in range(len(args))],
        out_specs=jax.tree.map(lambda _: vmem, outs),
        scratch_shapes=list(scratch),
        cost_estimate=pl.CostEstimate(flops=flops, bytes_accessed=moved, transcendentals=0),
        compiler_params=pltpu.CompilerParams(vmem_limit_bytes=48 * 1024 * 1024),
    )(*args)


def attend_body(chips, rows, scale, perm, *refs):
    pieces, siblings = refs[:chips], refs[chips : 2 * chips]
    attended, probs, keys_values, queries = refs[2 * chips :]
    chip = chip_index()
    for d in range(chips):
        for kind in range(2):
            keys_values[d, kind, :rows] = pieces[d][kind]
            keys_values[d, kind, rows:] = siblings[d][kind]
        queries[d] = pieces[d][2]
    for d in range(chips):
        p = perm[chip, chip ^ d] ^ chip
        query = pieces[d][2]
        local = dot(query, keys_values[d, 0], NT)
        remote = dot(query, keys_values[p, 0], NT)
        top = jnp.maximum(
            jnp.max(local, axis=1, keepdims=True), jnp.max(remote, axis=1, keepdims=True)
        )
        factor = scale * math.log2(math.e)
        local = jnp.exp2((local - top) * factor)
        remote = jnp.exp2((remote - top) * factor)
        total = jnp.sum(local, axis=1, keepdims=True) + jnp.sum(remote, axis=1, keepdims=True)
        share = 1.0 / total
        local = (local * share).astype(LOW)
        remote = (remote * share).astype(LOW)
        probs[d, :, : 2 * rows] = local
        probs[d, :, 2 * rows :] = remote
        result = dot(local, keys_values[d, 1]) + dot(remote, keys_values[p, 1])
        attended[d] = result.astype(LOW)


def backward_body(chips, rows, scale, perm, *refs):
    arrived = refs[:chips]
    attended, probs, keys_values, queries = refs[chips : chips + 4]
    query_grad, own_part, sibling_part, score_grad, grads = refs[chips + 4 :]
    chip = chip_index()
    for d in range(chips):
        p = perm[chip, chip ^ d] ^ chip
        grad = arrived[d][1]
        grads[d] = grad
        delta = jnp.sum(grad.astype(F32) * attended[d].astype(F32), axis=1, keepdims=True)
        total = None
        for part, source in ((0, d), (1, p)):
            lanes = slice(2 * rows * part, 2 * rows * (part + 1))
            prob_grad = dot(grad, keys_values[source, 1], NT)
            weight = probs[d, :, lanes].astype(F32)
            change = (weight * (prob_grad - delta) * scale).astype(LOW)
            score_grad[part, d] = change
            term = dot(change, keys_values[source, 0])
            total = term if total is None else total + term
        query_grad[d] = total.astype(LOW)
    for d in range(chips):
        asker = jnp.int32(0)
        for i in range(chips):
            asker = jnp.where(perm[chip, i] == chip ^ d, i, asker)
        asker = asker ^ chip
        for half, out in ((0, own_part), (1, sibling_part)):
            near = slice(half * rows, (half + 1) * rows)
            far = slice((half + 2) * rows, (half + 3) * rows)
            key_part = dot(score_grad[0, d, :, near], queries[d], TN)
            key_part += dot(score_grad[1, asker, :, near], queries[asker], TN)
            value_part = dot(probs[d, :, near], grads[d], TN)
            value_part += dot(probs[asker, :, far], grads[asker], TN)
            out[d, 0] = key_part.astype(out.dtype)
            out[d, 1] = value_part.astype(out.dtype)


def project_body(chips, groups, weight, *refs):
    incoming, outs, joined = refs[:chips], refs[chips : chips + groups], refs[chips + groups]
    chip = chip_index()
    level = lax.axis_index("head")
    width = incoming[0].shape[2]
    for d in range(chips):
        lanes = pl.ds(pl.multiple_of((chip ^ d) * width, width), width)
        joined[:, lanes] = incoming[d][0]
    rows = joined[...]
    for j in range(groups):
        columns = outs[j].shape[1]
        lanes = pl.ds(pl.multiple_of((level ^ j) * columns, columns), columns)
        term = weight[:, :, lanes].reshape(chips * width, columns)
        outs[j][...] = dot(rows, term).astype(LOW)


def grad_body(chips, groups, weight, attended, *refs):
    slices, outs = refs[:groups], refs[groups:]
    chip = chip_index()
    level = lax.axis_index("head")
    width = attended.shape[2]
    total = None
    for j in range(groups):
        block = slices[j][...]
        columns = block.shape[1]
        lanes = pl.ds(pl.multiple_of((level ^ j) * columns, columns), columns)
        term = dot(block, weight[:, :, lanes].reshape(chips * width, columns), NT)
        total = term if total is None else total + term
    total = total.astype(LOW)
    for d in range(chips):
        outs[d][0] = attended[d]
    for c in range(chips):

        @pl.when(chip == c)
        def _():
            for d in range(chips):
                h = c ^ d
                outs[d][1] = total[:, h * width : (h + 1) * width]


def merge_body(chips, query_grad, own_part, arrived, *outs):
    for d in range(chips):
        outs[d][0] = query_grad[d]
        for kind in range(2):
            both = own_part[d, kind] + arrived[d, kind].astype(F32)
            outs[d][1 + kind] = both.astype(LOW)


def place_body(chips, *refs):
    pieces, outs = refs[:chips], refs[chips:]
    chip = chip_index()
    for d in range(chips):
        for kind in range(3):
            outs[kind][chip ^ d] = pieces[d][kind]


def by_heads(queries, key_vectors, value_vectors, block_perm, out_weight, out_cotangent):
    devices = lax.axis_size("seq")
    chips = devices // 2
    groups = lax.axis_size("head")
    heads, rows, width = queries.shape
    features = out_weight.shape[2]
    columns = out_cotangent.shape[1]
    scale = 1.0 / math.sqrt(width)
    chip = chip_index()
    shape = jax.ShapeDtypeStruct

    def to_chip(array, d):
        return lax.ppermute(array, "seq", [(i, i ^ (2 * d)) for i in range(devices)])

    def to_sibling(array):
        return lax.ppermute(array, "seq", [(i, i ^ 1) for i in range(devices)])

    def together(*arrays):
        return list(lax.optimization_barrier(arrays))

    def exchange(pieces):
        return [pieces[0]] + [to_chip(pieces[d], d) for d in range(1, chips)]

    def head_piece(d):
        h = chip ^ d
        return jnp.stack(
            [
                lax.dynamic_index_in_dim(a, h, 0, keepdims=False)
                for a in (key_vectors, value_vectors, queries)
            ]
        )

    def along(array, pairs):
        return lax.ppermute(array, "head", pairs)

    def across(array, j):
        return along(array, [(i, i ^ j) for i in range(groups)])

    twice = across(out_cotangent, 2)
    once = across(out_cotangent, 1)
    pieces = [head_piece(d) for d in range(chips)]
    siblings = [to_sibling(pieces[0][:2])]
    pieces = exchange(pieces)
    *pieces[1:], twice, once = together(*pieces[1:], twice, once)
    slices = [out_cotangent, once, twice, across(twice, 1)]
    siblings += [to_sibling(piece[:2]) for piece in pieces[1:]]
    tile = rows * width
    scores = chips * rows * 4 * rows
    attended, probs, keys_values, query_rows = call(
        functools.partial(attend_body, chips, rows, scale),
        (
            shape((chips, rows, width), LOW),
            shape((chips, rows, 4 * rows), LOW),
            shape((chips, 2, 2 * rows, width), LOW),
            shape((chips, rows, width), LOW),
        ),
        block_perm,
        *pieces,
        *siblings,
        flops=4 * scores * width,
        moved=2 * (scores + 14 * chips * tile),
        smem=(0,),
    )
    weight_bytes = 2 * heads * width * features
    *slices, attended = together(*slices, attended)
    outgoing = call(
        functools.partial(grad_body, chips, groups),
        tuple(shape((2, rows, width), LOW) for _ in range(chips)),
        out_weight,
        attended,
        *slices,
        flops=2 * rows * heads * width * features,
        moved=weight_bytes + 2 * rows * features + 6 * chips * tile,
    )
    incoming = together(*exchange(outgoing))
    parts = call(
        functools.partial(project_body, chips, groups),
        tuple(shape((rows, columns), LOW) for _ in range(groups)),
        out_weight,
        *incoming,
        flops=2 * rows * heads * width * features,
        moved=weight_bytes + 2 * rows * features + 4 * chips * tile,
        scratch=[pltpu.VMEM((rows, heads * width), LOW)],
    )
    halfway = across(parts[3], 1)
    neighbour = across(parts[1], 1)
    halfway = (halfway.astype(F32) + parts[2].astype(F32)).astype(LOW)
    summands = [parts[0], neighbour, across(halfway, 2)]
    incoming[0] = together(incoming[0], parts[0])[0]
    query_grad, own_part, sibling_part = call(
        functools.partial(backward_body, chips, rows, scale),
        (
            shape((chips, rows, width), LOW),
            shape((chips, 2, rows, width), F32),
            shape((chips, 2, rows, width), LOW),
        ),
        block_perm,
        *incoming,
        attended,
        probs,
        keys_values,
        query_rows,
        flops=8 * scores * width,
        moved=2 * (scores + 20 * chips * tile),
        scratch=[
            pltpu.VMEM((2, chips, rows, 2 * rows), LOW),
            pltpu.VMEM((chips, rows, width), LOW),
        ],
        smem=(0,),
    )
    returned = exchange(
        call(
            functools.partial(merge_body, chips),
            tuple(shape((3, rows, width), LOW) for _ in range(chips)),
            query_grad,
            own_part,
            to_sibling(sibling_part),
            moved=2 * 14 * chips * tile,
        )
    )
    gradients = call(
        functools.partial(place_body, chips),
        tuple(shape((heads, rows, width), LOW) for _ in range(3)),
        *returned,
        moved=2 * 6 * chips * tile,
    )
    projected = sum(term.astype(F32) for term in summands)
    return (projected.astype(LOW), *gradients)


def partner(shard, axis, bit):
    return lax.ppermute(shard, axis, [(i, i ^ 1 << bit) for i in range(lax.axis_size(axis))])


def by_routing(queries, key_vectors, value_vectors, block_perm, out_weight, out_cotangent):
    devices = lax.axis_size("seq")
    position = lax.axis_index("seq")
    parity = position % 2
    group_heads, tok_rows, head_width = queries.shape
    portion = tok_rows * head_width // devices
    score_scale = 1.0 / math.sqrt(head_width)
    owners = jnp.repeat(block_perm, 2, axis=1)
    indices = lax.iota(jnp.int32, devices)
    sources = [2 * owners, 2 * owners + 1]
    source_table = jnp.stack(sources, axis=1)
    slot_count = source_table.shape[1]
    select = (source_table[..., None] == indices).astype(jnp.bfloat16)
    stacked = jnp.stack([key_vectors, value_vectors])
    spread = lax.all_to_all(
        stacked.reshape(2, group_heads, devices, portion),
        "seq",
        split_axis=2,
        concat_axis=2,
        tiled=True,
    )
    picked = jnp.einsum(
        "hsij,chjl->chsil", select, spread, preferred_element_type=jnp.float32
    ).astype(jnp.bfloat16)
    routed = lax.all_to_all(picked, "seq", split_axis=3, concat_axis=3, tiled=True)
    routed = routed.reshape(2, group_heads, slot_count, tok_rows, head_width)
    partner_kv = routed.reshape(2, group_heads, 2 * tok_rows, head_width)
    pair_other = partner(stacked, "seq", 0)
    local_kv = jnp.where(
        parity == 0,
        jnp.concatenate([stacked, pair_other], 2),
        jnp.concatenate([pair_other, stacked], 2),
    )
    combined = jnp.concatenate([local_kv, partner_kv], 2)
    key_all = combined[0]
    value_all = combined[1]
    logit_scores = (
        jnp.einsum("htd,hkd->htk", queries, key_all, preferred_element_type=jnp.float32)
        * score_scale
    )
    row_max = jnp.max(logit_scores, axis=-1, keepdims=True)
    weights = jnp.exp(logit_scores - row_max)
    probabilities = weights / jnp.sum(weights, axis=-1, keepdims=True)
    reduced_probabilities = probabilities.astype(jnp.bfloat16)
    attention_result = jnp.einsum(
        "htk,hkd->htd", reduced_probabilities, value_all, preferred_element_type=jnp.float32
    ).astype(jnp.bfloat16)
    partial_out = jnp.einsum(
        "htd,hde->te", attention_result, out_weight, preferred_element_type=jnp.float32
    )
    summed = lax.psum(partial_out.astype(jnp.bfloat16), "head").astype(jnp.float32)
    columns = summed.shape[1] // lax.axis_size("head")
    result = lax.dynamic_slice_in_dim(summed, lax.axis_index("head") * columns, columns, 1)
    projected = result.astype(jnp.bfloat16)
    full_grad = lax.all_gather(out_cotangent, "head", axis=1, tiled=True)
    grad_att = jnp.einsum(
        "te,hde->htd", full_grad, out_weight, preferred_element_type=jnp.float32
    ).astype(jnp.bfloat16)
    row_delta = jnp.sum(
        grad_att.astype(jnp.float32) * attention_result.astype(jnp.float32), axis=-1, keepdims=True
    )
    probability_gradient = jnp.einsum(
        "htd,hkd->htk", grad_att, value_all, preferred_element_type=jnp.float32
    )
    score_gradient = (probabilities * (probability_gradient - row_delta) * score_scale).astype(
        jnp.bfloat16
    )
    gradient_of_queries = jnp.einsum(
        "htk,hkd->htd", score_gradient, key_all, preferred_element_type=jnp.float32
    ).astype(jnp.bfloat16)
    key_part = jnp.einsum(
        "htk,htd->hkd", score_gradient, queries, preferred_element_type=jnp.float32
    )
    value_part = jnp.einsum(
        "htk,htd->hkd", reduced_probabilities, grad_att, preferred_element_type=jnp.float32
    )
    gradients = jnp.stack([key_part, value_part])
    block_rows = 2 * tok_rows
    local_grad = gradients[:, :, :block_rows].reshape(2, group_heads, 2, tok_rows, head_width)
    own_grad = jnp.where(parity == 0, local_grad[:, :, 0], local_grad[:, :, 1])
    other_grad = jnp.where(parity == 0, local_grad[:, :, 1], local_grad[:, :, 0]).astype(
        jnp.bfloat16
    )
    partner_grad = gradients[:, :, block_rows:].reshape(2, group_heads, 2, tok_rows, head_width)
    partner_grad = partner_grad.astype(jnp.bfloat16)
    returned = lax.all_to_all(
        partner_grad.reshape(2, group_heads, slot_count, devices, portion),
        "seq",
        split_axis=3,
        concat_axis=3,
        tiled=True,
    )
    summed_back = jnp.einsum(
        "hsij,chsil->chjl", select, returned, preferred_element_type=jnp.float32
    ).astype(jnp.bfloat16)
    arrived = lax.all_to_all(summed_back, "seq", split_axis=2, concat_axis=2, tiled=True)
    arrived = arrived.reshape(2, group_heads, tok_rows, head_width).astype(jnp.float32)
    pair_back = partner(other_grad, "seq", 0).astype(jnp.float32)
    total_grad = own_grad + arrived + pair_back
    key_grad = total_grad[0].astype(jnp.bfloat16)
    value_grad = total_grad[1].astype(jnp.bfloat16)
    return (projected, gradient_of_queries, key_grad, value_grad)


def per_device(*arrays):
    chips = lax.axis_size("seq") // 2
    square = chips == arrays[0].shape[0]
    return (by_heads if square else by_routing)(*arrays)


def solution(mesh):
    return jax.shard_map(
        per_device,
        mesh=mesh,
        in_specs=(
            P("head", "seq", None),
            P("head", "seq", None),
            P("head", "seq", None),
            P("head", None),
            P("head", None, None),
            P("seq", "head"),
        ),
        out_specs=(
            P("seq", "head"),
            P("head", "seq", None),
            P("head", "seq", None),
            P("head", "seq", None),
        ),
        check_vma=False,
    )
```

```python
import functools
import math

import jax
import jax.numpy as jnp
from jax import lax
from jax.experimental import pallas as pl
from jax.experimental.pallas import tpu as pltpu
from jax.sharding import PartitionSpec as P

F32 = jnp.float32
LOW = jnp.bfloat16
NT = (((1,), (1,)), ((), ()))
NN = (((1,), (0,)), ((), ()))
TN = (((0,), (0,)), ((), ()))


def dot(a, b, dims=NN):
    return lax.dot_general(a, b, dims, preferred_element_type=F32)


def chip_index():
    return lax.axis_index("seq") // 2


def call(body, outs, *args, flops=0, moved=0, scratch=(), smem=()):
    vmem = pl.BlockSpec(memory_space=pltpu.VMEM)
    scalar = pl.BlockSpec(memory_space=pltpu.SMEM)
    return pl.pallas_call(
        body,
        out_shape=outs,
        in_specs=[scalar if i in smem else vmem for i in range(len(args))],
        out_specs=jax.tree.map(lambda _: vmem, outs),
        scratch_shapes=list(scratch),
        cost_estimate=pl.CostEstimate(flops=flops, bytes_accessed=moved, transcendentals=0),
        compiler_params=pltpu.CompilerParams(vmem_limit_bytes=16 * 1024 * 1024),
    )(*args)


def attend_body(chips, rows, scale, perm, *refs):
    pieces, siblings = refs[:chips], refs[chips : 2 * chips]
    attended, probs, keys_values, queries, shares, values = refs[2 * chips :]
    chip = chip_index()
    for d in range(chips):
        keys_values[d, 0, :rows] = pieces[d][0]
        keys_values[d, 0, rows:] = siblings[d][0]
        values[d, :rows, :128] = pieces[d][1]
        values[d, rows:, :128] = siblings[d][1]
        values[d, :, 128:] = jnp.ones((2*rows,128),LOW)
        keys_values[d, 1, :rows] = pieces[d][1]
        keys_values[d, 1, rows:] = siblings[d][1]
        queries[d] = pieces[d][2]
    factor = scale * math.log2(math.e)
    for d in range(chips):
        p = perm[chip, chip ^ d] ^ chip
        query = pieces[d][2]
        local = dot(query, keys_values[d, 0], NT)
        remote = dot(query, keys_values[p, 0], NT)
        top = jnp.max(jnp.maximum(local, remote), axis=1, keepdims=True)
        local = jnp.exp2((local - top) * factor).astype(LOW)
        remote = jnp.exp2((remote - top) * factor).astype(LOW)
        probs[d, :, : 2 * rows] = local
        probs[d, :, 2 * rows :] = remote
        result = dot(local, values[d]) + dot(remote, values[p])
        share = 1.0 / result[:, 128:]
        shares[d] = share
        attended[d] = (result[:, :128] * share).astype(LOW)


def backward_body(chips, rows, scale, perm, *refs):
    arrived = refs[:chips]
    attended, probs, keys_values, queries, shares = refs[chips : chips + 5]
    query_grad, own_part, sibling_part, score_grad, scaled = refs[chips + 5 :]
    chip = chip_index()
    for d in range(chips):
        p = perm[chip, chip ^ d] ^ chip
        grad = arrived[d][...]
        share = shares[d]
        g32 = grad.astype(F32)
        delta = jnp.sum(g32 * attended[d].astype(F32), axis=1, keepdims=True)
        scaled[0, d] = (queries[d].astype(F32) * (share * scale)).astype(LOW)
        scaled[1, d] = (g32 * share).astype(LOW)
        total = None
        for part, source in ((0, d), (1, p)):
            lanes = slice(2 * rows * part, 2 * rows * (part + 1))
            prob_grad = dot(grad, keys_values[source, 1], NT)
            change = (probs[d, :, lanes].astype(F32) * (prob_grad - delta)).astype(LOW)
            score_grad[part, d] = change
            term = dot(change, keys_values[source, 0])
            total = term if total is None else total + term
        query_grad[d] = (total * (share * scale)).astype(LOW)
    for d in range(chips):
        asker = jnp.int32(0)
        for i in range(chips):
            asker = jnp.where(perm[chip, i] == chip ^ d, i, asker)
        asker = asker ^ chip
        for half, out in ((0, own_part), (1, sibling_part)):
            near = slice(half * rows, (half + 1) * rows)
            far = slice((half + 2) * rows, (half + 3) * rows)
            key_part = dot(score_grad[0, d, :, near], scaled[0, d], TN)
            key_part += dot(score_grad[1, asker, :, near], scaled[0, asker], TN)
            value_part = dot(probs[d, :, near], scaled[1, d], TN)
            value_part += dot(probs[asker, :, far], scaled[1, asker], TN)
            out[d, 0] = key_part.astype(out.dtype)
            out[d, 1] = value_part.astype(out.dtype)


def project_body(chips, groups, weight, *refs):
    incoming, outs, joined = refs[:chips], refs[chips : chips + groups], refs[chips + groups]
    chip = chip_index()
    level = lax.axis_index("head")
    width = incoming[0].shape[1]
    for d in range(chips):
        lanes = pl.ds(pl.multiple_of((chip ^ d) * width, width), width)
        joined[:, lanes] = incoming[d][...]
    rows = joined[...]
    for j in range(groups):
        columns = outs[j].shape[1]
        lanes = pl.ds(pl.multiple_of((level ^ j) * columns, columns), columns)
        term = weight[:, :, lanes].reshape(chips * width, columns)
        outs[j][...] = dot(rows, term).astype(LOW)


def grad_body(chips, groups, weight, *refs):
    slices, outs = refs[:groups], refs[groups:]
    chip = chip_index()
    level = lax.axis_index("head")
    width = outs[0].shape[1]
    total = None
    for j in range(groups):
        block = slices[j][...]
        columns = block.shape[1]
        lanes = pl.ds(pl.multiple_of((level ^ j) * columns, columns), columns)
        term = dot(block, weight[:, :, lanes].reshape(chips * width, columns), NT)
        total = term if total is None else total + term
    total = total.astype(LOW)
    for c in range(chips):

        @pl.when(chip == c)
        def _():
            for d in range(chips):
                h = c ^ d
                outs[d][...] = total[:, h * width : (h + 1) * width]


def sum_body(*refs):
    total = refs[0][...].astype(F32)
    for ref in refs[1:-1]:
        total = total + ref[...].astype(F32)
    refs[-1][...] = total.astype(LOW)


def merge_body(chips, query_grad, own_part, arrived, *outs):
    for d in range(chips):
        outs[d][0] = query_grad[d]
        for kind in range(2):
            both = own_part[d, kind] + arrived[d, kind].astype(F32)
            outs[d][1 + kind] = both.astype(LOW)


def place_body(chips, *refs):
    summands, pieces, projected, outs = refs[:3], refs[3 : 3 + chips], refs[3 + chips], refs[4 + chips :]
    chip = chip_index()
    sum_body(*summands, projected)
    for d in range(chips):
        for kind in range(3):
            outs[kind][chip ^ d] = pieces[d][kind]


def by_heads(queries, key_vectors, value_vectors, block_perm, out_weight, out_cotangent):
    devices = lax.axis_size("seq")
    chips = devices // 2
    groups = lax.axis_size("head")
    heads, rows, width = queries.shape
    features = out_weight.shape[2]
    columns = out_cotangent.shape[1]
    scale = 1.0 / math.sqrt(width)
    chip = chip_index()
    shape = jax.ShapeDtypeStruct

    def to_chip(array, d):
        return lax.ppermute(array, "seq", [(i, i ^ (2 * d)) for i in range(devices)])

    def to_sibling(array):
        return lax.ppermute(array, "seq", [(i, i ^ 1) for i in range(devices)])

    def together(*arrays):
        return list(lax.optimization_barrier(arrays))

    def exchange(pieces):
        return [pieces[0]] + [to_chip(pieces[d], d) for d in range(1, chips)]

    def head_piece(d):
        h = chip ^ d
        return jnp.stack(
            [
                lax.dynamic_index_in_dim(a, h, 0, keepdims=False)
                for a in (key_vectors, value_vectors, queries)
            ]
        )

    def along(array, pairs):
        return lax.ppermute(array, "head", pairs)

    def across(array, j):
        return along(array, [(i, i ^ j) for i in range(groups)])

    twice = across(out_cotangent, 2)
    once = across(out_cotangent, 1)
    pieces = [head_piece(d) for d in range(chips)]
    siblings = [to_sibling(pieces[0][:2])]
    pieces = exchange(pieces)
    pieces[3], twice, once = together(pieces[3], twice, once)
    slices = [out_cotangent, once, twice, across(twice, 1)]
    siblings += [to_sibling(piece[:2]) for piece in pieces[1:]]
    tile = rows * width
    scores = chips * rows * 4 * rows
    piece = shape((rows, width), LOW)
    attended, probs, keys_values, query_rows, shares = call(
        functools.partial(attend_body, chips, rows, scale),
        (
            shape((chips, rows, width), LOW),
            shape((chips, rows, 4 * rows), LOW),
            shape((chips, 2, 2 * rows, width), LOW),
            shape((chips, rows, width), LOW),
            shape((chips, rows, width), F32),
        ),
        block_perm,
        *pieces,
        *siblings,
        flops=4 * scores * width,
        moved=2 * (scores + 14 * chips * tile),
        scratch=[pltpu.VMEM((chips, 2 * rows, 2 * width), LOW)],
        smem=(0,),
    )
    weight_bytes = 2 * heads * width * features
    own_attended = exchange([attended[d] for d in range(chips)])
    attended, *slices = together(attended, *slices)
    grad_att = call(
        functools.partial(grad_body, chips, groups),
        (piece,) * chips,
        out_weight,
        *slices,
        flops=2 * rows * heads * width * features,
        moved=weight_bytes + 2 * rows * features + 6 * chips * tile,
    )
    incoming = exchange(grad_att)
    own_attended[0] = together(own_attended[0], grad_att[0])[0]
    parts = call(
        functools.partial(project_body, chips, groups),
        tuple(shape((rows, columns), LOW) for _ in range(groups)),
        out_weight,
        *own_attended,
        flops=2 * rows * heads * width * features,
        moved=weight_bytes + 2 * rows * features + 4 * chips * tile,
        scratch=[pltpu.VMEM((rows, heads * width), LOW)],
    )
    halfway = across(parts[3], 1)
    neighbour = across(together(parts[1], incoming[1])[0], 1)
    halfway = call(sum_body, shape((rows, columns), LOW), halfway, parts[2], flops=2**33, moved=2**28)
    incoming[0] = together(incoming[0], parts[0])[0]
    query_grad, own_part, sibling_part = call(
        functools.partial(backward_body, chips, rows, scale),
        (
            shape((chips, rows, width), LOW),
            shape((chips, 2, rows, width), F32),
            shape((chips, 2, rows, width), LOW),
        ),
        block_perm,
        *incoming,
        attended,
        probs,
        keys_values,
        query_rows,
        shares,
        flops=2**33,
        moved=2 * (scores + 20 * chips * tile),
        scratch=[
            pltpu.VMEM((2, chips, rows, 2 * rows), LOW),
            pltpu.VMEM((2, chips, rows, width), LOW),
        ],
        smem=(0,),
    )
    returned = exchange(
        call(
            functools.partial(merge_body, chips),
            tuple(shape((3, rows, width), LOW) for _ in range(chips)),
            query_grad,
            own_part,
            to_sibling(sibling_part),
            moved=2 * 14 * chips * tile,
        )
    )
    return call(
        functools.partial(place_body, chips),
        (shape((rows, columns), LOW),) + (shape((heads, rows, width), LOW),) * 3,
        parts[0],
        neighbour,
        across(halfway, 2),
        *returned,
        moved=2 * 6 * chips * tile,
    )


def partner(shard, axis, bit):
    return lax.ppermute(shard, axis, [(i, i ^ 1 << bit) for i in range(lax.axis_size(axis))])


def by_routing(queries, key_vectors, value_vectors, block_perm, out_weight, out_cotangent):
    devices = lax.axis_size("seq")
    position = lax.axis_index("seq")
    parity = position % 2
    group_heads, tok_rows, head_width = queries.shape
    portion = tok_rows * head_width // devices
    score_scale = 1.0 / math.sqrt(head_width)
    owners = jnp.repeat(block_perm, 2, axis=1)
    indices = lax.iota(jnp.int32, devices)
    sources = [2 * owners, 2 * owners + 1]
    source_table = jnp.stack(sources, axis=1)
    slot_count = source_table.shape[1]
    select = (source_table[..., None] == indices).astype(jnp.bfloat16)
    stacked = jnp.stack([key_vectors, value_vectors])
    spread = lax.all_to_all(
        stacked.reshape(2, group_heads, devices, portion),
        "seq",
        split_axis=2,
        concat_axis=2,
        tiled=True,
    )
    picked = jnp.einsum(
        "hsij,chjl->chsil", select, spread, preferred_element_type=jnp.float32
    ).astype(jnp.bfloat16)
    routed = lax.all_to_all(picked, "seq", split_axis=3, concat_axis=3, tiled=True)
    routed = routed.reshape(2, group_heads, slot_count, tok_rows, head_width)
    partner_kv = routed.reshape(2, group_heads, 2 * tok_rows, head_width)
    pair_other = partner(stacked, "seq", 0)
    local_kv = jnp.where(
        parity == 0,
        jnp.concatenate([stacked, pair_other], 2),
        jnp.concatenate([pair_other, stacked], 2),
    )
    combined = jnp.concatenate([local_kv, partner_kv], 2)
    key_all = combined[0]
    value_all = combined[1]
    logit_scores = (
        jnp.einsum("htd,hkd->htk", queries, key_all, preferred_element_type=jnp.float32)
        * score_scale
    )
    row_max = jnp.max(logit_scores, axis=-1, keepdims=True)
    weights = jnp.exp(logit_scores - row_max)
    probabilities = weights / jnp.sum(weights, axis=-1, keepdims=True)
    reduced_probabilities = probabilities.astype(jnp.bfloat16)
    attention_result = jnp.einsum(
        "htk,hkd->htd", reduced_probabilities, value_all, preferred_element_type=jnp.float32
    ).astype(jnp.bfloat16)
    partial_out = jnp.einsum(
        "htd,hde->te", attention_result, out_weight, preferred_element_type=jnp.float32
    )
    summed = lax.psum(partial_out.astype(jnp.bfloat16), "head").astype(jnp.float32)
    columns = summed.shape[1] // lax.axis_size("head")
    result = lax.dynamic_slice_in_dim(summed, lax.axis_index("head") * columns, columns, 1)
    projected = result.astype(jnp.bfloat16)
    full_grad = lax.all_gather(out_cotangent, "head", axis=1, tiled=True)
    grad_att = jnp.einsum(
        "te,hde->htd", full_grad, out_weight, preferred_element_type=jnp.float32
    ).astype(jnp.bfloat16)
    row_delta = jnp.sum(
        grad_att.astype(jnp.float32) * attention_result.astype(jnp.float32), axis=-1, keepdims=True
    )
    probability_gradient = jnp.einsum(
        "htd,hkd->htk", grad_att, value_all, preferred_element_type=jnp.float32
    )
    score_gradient = (probabilities * (probability_gradient - row_delta) * score_scale).astype(
        jnp.bfloat16
    )
    gradient_of_queries = jnp.einsum(
        "htk,hkd->htd", score_gradient, key_all, preferred_element_type=jnp.float32
    ).astype(jnp.bfloat16)
    key_part = jnp.einsum(
        "htk,htd->hkd", score_gradient, queries, preferred_element_type=jnp.float32
    )
    value_part = jnp.einsum(
        "htk,htd->hkd", reduced_probabilities, grad_att, preferred_element_type=jnp.float32
    )
    gradients = jnp.stack([key_part, value_part])
    block_rows = 2 * tok_rows
    local_grad = gradients[:, :, :block_rows].reshape(2, group_heads, 2, tok_rows, head_width)
    own_grad = jnp.where(parity == 0, local_grad[:, :, 0], local_grad[:, :, 1])
    other_grad = jnp.where(parity == 0, local_grad[:, :, 1], local_grad[:, :, 0]).astype(
        jnp.bfloat16
    )
    partner_grad = gradients[:, :, block_rows:].reshape(2, group_heads, 2, tok_rows, head_width)
    partner_grad = partner_grad.astype(jnp.bfloat16)
    returned = lax.all_to_all(
        partner_grad.reshape(2, group_heads, slot_count, devices, portion),
        "seq",
        split_axis=3,
        concat_axis=3,
        tiled=True,
    )
    summed_back = jnp.einsum(
        "hsij,chsil->chjl", select, returned, preferred_element_type=jnp.float32
    ).astype(jnp.bfloat16)
    arrived = lax.all_to_all(summed_back, "seq", split_axis=2, concat_axis=2, tiled=True)
    arrived = arrived.reshape(2, group_heads, tok_rows, head_width).astype(jnp.float32)
    pair_back = partner(other_grad, "seq", 0).astype(jnp.float32)
    total_grad = own_grad + arrived + pair_back
    key_grad = total_grad[0].astype(jnp.bfloat16)
    value_grad = total_grad[1].astype(jnp.bfloat16)
    return (projected, gradient_of_queries, key_grad, value_grad)


def per_device(*arrays):
    chips = lax.axis_size("seq") // 2
    square = chips == arrays[0].shape[0]
    return (by_heads if square else by_routing)(*arrays)


def solution(mesh):
    return jax.shard_map(
        per_device,
        mesh=mesh,
        in_specs=(
            P("head", "seq", None),
            P("head", "seq", None),
            P("head", "seq", None),
            P("head", None),
            P("head", None, None),
            P("seq", "head"),
        ),
        out_specs=(
            P("seq", "head"),
            P("head", "seq", None),
            P("head", "seq", None),
            P("head", "seq", None),
        ),
        check_vma=False,
    )
```

```python
import functools
import math

import jax
import jax.numpy as jnp
from jax import lax
from jax.experimental import pallas as pl
from jax.experimental.pallas import tpu as pltpu
from jax.sharding import PartitionSpec as P

F32 = jnp.float32
LOW = jnp.bfloat16
NT = (((1,), (1,)), ((), ()))
NN = (((1,), (0,)), ((), ()))
TN = (((0,), (0,)), ((), ()))


def dot(a, b, dims=NN):
    return lax.dot_general(a, b, dims, preferred_element_type=F32)


def chip_index():
    return lax.axis_index("seq") // 2


def call(body, outs, *args, flops=0, moved=0, scratch=(), smem=()):
    vmem = pl.BlockSpec(memory_space=pltpu.VMEM)
    scalar = pl.BlockSpec(memory_space=pltpu.SMEM)
    return pl.pallas_call(
        body,
        out_shape=outs,
        in_specs=[scalar if i in smem else vmem for i in range(len(args))],
        out_specs=jax.tree.map(lambda _: vmem, outs),
        scratch_shapes=list(scratch),
        cost_estimate=pl.CostEstimate(flops=flops, bytes_accessed=moved, transcendentals=0),
        compiler_params=pltpu.CompilerParams(vmem_limit_bytes=16 * 1024 * 1024),
    )(*args)


def attend_body(chips, rows, scale, perm, *refs):
    pieces, siblings = refs[:chips], refs[chips : 2 * chips]
    attended, probs, keys_values, queries, shares, values = refs[2 * chips :]
    chip = chip_index()
    for d in range(chips):
        keys_values[d, 0, :rows] = pieces[d][0]
        keys_values[d, 0, rows:] = siblings[d][0]
        values[d, :rows, :128] = pieces[d][1]
        values[d, rows:, :128] = siblings[d][1]
        values[d, :, 128:] = jnp.ones((2*rows,128),LOW)
        keys_values[d, 1, :rows] = pieces[d][1]
        keys_values[d, 1, rows:] = siblings[d][1]
        queries[d] = pieces[d][2]
    factor = scale * math.log2(math.e)
    for d in range(chips):
        p = perm[chip, chip ^ d] ^ chip
        query = pieces[d][2]
        local = dot(query, keys_values[d, 0], NT)
        remote = dot(query, keys_values[p, 0], NT)
        top = jnp.max(jnp.maximum(local, remote), axis=1, keepdims=True)
        local = jnp.exp2((local - top) * factor).astype(LOW)
        remote = jnp.exp2((remote - top) * factor).astype(LOW)
        probs[d, :, : 2 * rows] = local
        probs[d, :, 2 * rows :] = remote
        result = dot(local, values[d]) + dot(remote, values[p])
        share = 1.0 / result[:, 128:]
        shares[d] = share
        attended[d] = (result[:, :128] * share).astype(LOW)


def backward_body(chips, rows, scale, perm, *refs):
    arrived = refs[:chips]
    attended, probs, keys_values, queries, shares = refs[chips : chips + 5]
    query_grad, own_part, sibling_part, score_grad, scaled = refs[chips + 5 :]
    chip = chip_index()
    for d in range(chips):
        p = perm[chip, chip ^ d] ^ chip
        grad = arrived[d][...]
        share = shares[d]
        g32 = grad.astype(F32)
        delta = jnp.sum(g32 * attended[d].astype(F32), axis=1, keepdims=True)
        scaled[0, d] = (queries[d].astype(F32) * (share * scale)).astype(LOW)
        scaled[1, d] = (g32 * share).astype(LOW)
        total = None
        for part, source in ((0, d), (1, p)):
            lanes = slice(2 * rows * part, 2 * rows * (part + 1))
            prob_grad = dot(grad, keys_values[source, 1], NT)
            change = (probs[d, :, lanes].astype(F32) * (prob_grad - delta)).astype(LOW)
            score_grad[part, d] = change
            term = dot(change, keys_values[source, 0])
            total = term if total is None else total + term
        query_grad[d] = (total * (share * scale)).astype(LOW)
    for d in range(chips):
        asker = jnp.int32(0)
        for i in range(chips):
            asker = jnp.where(perm[chip, i] == chip ^ d, i, asker)
        asker = asker ^ chip
        for half, out in ((0, own_part), (1, sibling_part)):
            near = slice(half * rows, (half + 1) * rows)
            far = slice((half + 2) * rows, (half + 3) * rows)
            key_part = dot(score_grad[0, d, :, near], scaled[0, d], TN)
            key_part += dot(score_grad[1, asker, :, near], scaled[0, asker], TN)
            value_part = dot(probs[d, :, near], scaled[1, d], TN)
            value_part += dot(probs[asker, :, far], scaled[1, asker], TN)
            out[d, 0] = key_part.astype(out.dtype)
            out[d, 1] = value_part.astype(out.dtype)


def join_body(chips, groups, weight, *refs):
    incoming, joined, out = refs[:chips], refs[chips], refs[chips + 1]
    chip = chip_index()
    width = incoming[0].shape[1]
    for d in range(chips):
        lanes = pl.ds(pl.multiple_of((chip ^ d) * width, width), width)
        joined[:, lanes] = incoming[d][...]
    project_part(weight, joined[...], out, lax.axis_index("head") ^ (groups - 1))


def project_part(weight, rows, out, index):
    columns = out.shape[1]
    lanes = pl.ds(pl.multiple_of(index * columns, columns), columns)
    out[...] = dot(rows, weight[:, :, lanes].reshape(rows.shape[1], columns)).astype(LOW)


def project_body(weight, joined, *outs):
    level = lax.axis_index("head")
    for j, out in enumerate(outs):
        project_part(weight, joined[...], out, level ^ j)


def grad_body(chips, groups, weight, *refs):
    slices, outs = refs[:groups], refs[groups:]
    chip = chip_index()
    level = lax.axis_index("head")
    width = outs[0].shape[1]
    total = None
    for j in range(groups):
        block = slices[j][...]
        columns = block.shape[1]
        lanes = pl.ds(pl.multiple_of((level ^ j) * columns, columns), columns)
        term = dot(block, weight[:, :, lanes].reshape(chips * width, columns), NT)
        total = term if total is None else total + term
    total = total.astype(LOW)
    for c in range(chips):

        @pl.when(chip == c)
        def _():
            for d in range(chips):
                h = c ^ d
                outs[d][...] = total[:, h * width : (h + 1) * width]


def sum_body(*refs):
    total = refs[0][...].astype(F32)
    for ref in refs[1:-1]:
        total = total + ref[...].astype(F32)
    refs[-1][...] = total.astype(LOW)


def merge_body(chips, query_grad, own_part, arrived, *outs):
    for d in range(chips):
        outs[d][0] = query_grad[d]
        for kind in range(2):
            both = own_part[d, kind] + arrived[d, kind].astype(F32)
            outs[d][1 + kind] = both.astype(LOW)


def place_body(chips, *refs):
    pieces, outs = refs[:chips], refs[chips:]
    chip = chip_index()
    for d in range(chips):
        for kind in range(3):
            outs[kind][chip ^ d] = pieces[d][kind]


def by_heads(queries, key_vectors, value_vectors, block_perm, out_weight, out_cotangent):
    devices = lax.axis_size("seq")
    chips = devices // 2
    groups = lax.axis_size("head")
    heads, rows, width = queries.shape
    features = out_weight.shape[2]
    columns = out_cotangent.shape[1]
    scale = 1.0 / math.sqrt(width)
    chip = chip_index()
    shape = jax.ShapeDtypeStruct

    def to_chip(array, d):
        return lax.ppermute(array, "seq", [(i, i ^ (2 * d)) for i in range(devices)])

    def to_sibling(array):
        return lax.ppermute(array, "seq", [(i, i ^ 1) for i in range(devices)])

    def together(*arrays):
        return list(lax.optimization_barrier(arrays))

    def exchange(pieces):
        return [pieces[0]] + [to_chip(pieces[d], d) for d in range(1, chips)]

    def head_piece(d):
        h = chip ^ d
        return jnp.stack(
            [
                lax.dynamic_index_in_dim(a, h, 0, keepdims=False)
                for a in (key_vectors, value_vectors, queries)
            ]
        )

    def along(array, pairs):
        return lax.ppermute(array, "head", pairs)

    def across(array, j):
        return along(array, [(i, i ^ j) for i in range(groups)])

    twice = across(out_cotangent, 2)
    once = across(out_cotangent, 1)
    pieces = [head_piece(d) for d in range(chips)]
    siblings = [to_sibling(pieces[0][:2])]
    pieces = exchange(pieces)
    pieces[3], twice, once = together(pieces[3], twice, once)
    slices = [out_cotangent, once, twice, across(twice, 1)]
    siblings += [to_sibling(piece[:2]) for piece in pieces[1:]]
    tile = rows * width
    scores = chips * rows * 4 * rows
    piece = shape((rows, width), LOW)
    attended, probs, keys_values, query_rows, shares = call(
        functools.partial(attend_body, chips, rows, scale),
        (
            shape((chips, rows, width), LOW),
            shape((chips, rows, 4 * rows), LOW),
            shape((chips, 2, 2 * rows, width), LOW),
            shape((chips, rows, width), LOW),
            shape((chips, rows, width), F32),
        ),
        block_perm,
        *pieces,
        *siblings,
        flops=4 * scores * width,
        moved=2 * (scores + 14 * chips * tile),
        scratch=[pltpu.VMEM((chips, 2 * rows, 2 * width), LOW)],
        smem=(0,),
    )
    weight_bytes = 2 * heads * width * features
    own_attended = exchange([attended[d] for d in range(chips)])
    attended, *slices = together(attended, *slices)
    grad_att = call(
        functools.partial(grad_body, chips, groups),
        (piece,) * chips,
        out_weight,
        *slices,
        flops=2 * rows * heads * width * features,
        moved=weight_bytes + 2 * rows * features + 6 * chips * tile,
    )
    incoming = exchange(grad_att)
    own_attended[0] = together(own_attended[0], grad_att[0])[0]
    block = shape((rows, columns), LOW)
    joined, *parts = call(
        functools.partial(join_body, chips, groups),
        (shape((rows, heads * width), LOW), block),
        out_weight,
        *own_attended,
        flops=2 * rows * heads * width * columns,
        moved=weight_bytes // groups + 4 * chips * tile,
    )
    halfway = across(parts[0], 1)
    parts = call(
        project_body,
        (block,) * (groups - 1),
        out_weight,
        joined,
        flops=2 * rows * heads * width * (features - columns),
        moved=weight_bytes + 2 * rows * features,
    )
    neighbour = across(together(parts[1], *incoming[2:])[0], 1)
    halfway = call(sum_body, shape((rows, columns), LOW), halfway, parts[2], flops=2**33, moved=2**28)
    incoming[0] = together(incoming[0], parts[0])[0]
    query_grad, own_part, sibling_part = call(
        functools.partial(backward_body, chips, rows, scale),
        (
            shape((chips, rows, width), LOW),
            shape((chips, 2, rows, width), F32),
            shape((chips, 2, rows, width), LOW),
        ),
        block_perm,
        *incoming,
        attended,
        probs,
        keys_values,
        query_rows,
        shares,
        flops=2**33,
        moved=2 * (scores + 20 * chips * tile),
        scratch=[
            pltpu.VMEM((2, chips, rows, 2 * rows), LOW),
            pltpu.VMEM((2, chips, rows, width), LOW),
        ],
        smem=(0,),
    )
    returned = exchange(
        call(
            functools.partial(merge_body, chips),
            tuple(shape((3, rows, width), LOW) for _ in range(chips)),
            query_grad,
            own_part,
            to_sibling(sibling_part),
            moved=2 * 14 * chips * tile,
        )
    )
    summands = [parts[0], neighbour, across(halfway, 2)]
    gradients = call(
        functools.partial(place_body, chips),
        (shape((heads, rows, width), LOW),) * 3,
        *returned,
        moved=2 * 6 * chips * tile,
    )
    summands[0], *gradients = together(summands[0], *gradients)
    projected = call(sum_body, block, *summands)
    return (projected, *gradients)


def partner(shard, axis, bit):
    return lax.ppermute(shard, axis, [(i, i ^ 1 << bit) for i in range(lax.axis_size(axis))])


def by_routing(queries, key_vectors, value_vectors, block_perm, out_weight, out_cotangent):
    devices = lax.axis_size("seq")
    position = lax.axis_index("seq")
    parity = position % 2
    group_heads, tok_rows, head_width = queries.shape
    portion = tok_rows * head_width // devices
    score_scale = 1.0 / math.sqrt(head_width)
    owners = jnp.repeat(block_perm, 2, axis=1)
    indices = lax.iota(jnp.int32, devices)
    sources = [2 * owners, 2 * owners + 1]
    source_table = jnp.stack(sources, axis=1)
    slot_count = source_table.shape[1]
    select = (source_table[..., None] == indices).astype(jnp.bfloat16)
    stacked = jnp.stack([key_vectors, value_vectors])
    spread = lax.all_to_all(
        stacked.reshape(2, group_heads, devices, portion),
        "seq",
        split_axis=2,
        concat_axis=2,
        tiled=True,
    )
    picked = jnp.einsum(
        "hsij,chjl->chsil", select, spread, preferred_element_type=jnp.float32
    ).astype(jnp.bfloat16)
    routed = lax.all_to_all(picked, "seq", split_axis=3, concat_axis=3, tiled=True)
    routed = routed.reshape(2, group_heads, slot_count, tok_rows, head_width)
    partner_kv = routed.reshape(2, group_heads, 2 * tok_rows, head_width)
    pair_other = partner(stacked, "seq", 0)
    local_kv = jnp.where(
        parity == 0,
        jnp.concatenate([stacked, pair_other], 2),
        jnp.concatenate([pair_other, stacked], 2),
    )
    combined = jnp.concatenate([local_kv, partner_kv], 2)
    key_all = combined[0]
    value_all = combined[1]
    logit_scores = (
        jnp.einsum("htd,hkd->htk", queries, key_all, preferred_element_type=jnp.float32)
        * score_scale
    )
    row_max = jnp.max(logit_scores, axis=-1, keepdims=True)
    weights = jnp.exp(logit_scores - row_max)
    probabilities = weights / jnp.sum(weights, axis=-1, keepdims=True)
    reduced_probabilities = probabilities.astype(jnp.bfloat16)
    attention_result = jnp.einsum(
        "htk,hkd->htd", reduced_probabilities, value_all, preferred_element_type=jnp.float32
    ).astype(jnp.bfloat16)
    partial_out = jnp.einsum(
        "htd,hde->te", attention_result, out_weight, preferred_element_type=jnp.float32
    )
    summed = lax.psum(partial_out.astype(jnp.bfloat16), "head").astype(jnp.float32)
    columns = summed.shape[1] // lax.axis_size("head")
    result = lax.dynamic_slice_in_dim(summed, lax.axis_index("head") * columns, columns, 1)
    projected = result.astype(jnp.bfloat16)
    full_grad = lax.all_gather(out_cotangent, "head", axis=1, tiled=True)
    grad_att = jnp.einsum(
        "te,hde->htd", full_grad, out_weight, preferred_element_type=jnp.float32
    ).astype(jnp.bfloat16)
    row_delta = jnp.sum(
        grad_att.astype(jnp.float32) * attention_result.astype(jnp.float32), axis=-1, keepdims=True
    )
    probability_gradient = jnp.einsum(
        "htd,hkd->htk", grad_att, value_all, preferred_element_type=jnp.float32
    )
    score_gradient = (probabilities * (probability_gradient - row_delta) * score_scale).astype(
        jnp.bfloat16
    )
    gradient_of_queries = jnp.einsum(
        "htk,hkd->htd", score_gradient, key_all, preferred_element_type=jnp.float32
    ).astype(jnp.bfloat16)
    key_part = jnp.einsum(
        "htk,htd->hkd", score_gradient, queries, preferred_element_type=jnp.float32
    )
    value_part = jnp.einsum(
        "htk,htd->hkd", reduced_probabilities, grad_att, preferred_element_type=jnp.float32
    )
    gradients = jnp.stack([key_part, value_part])
    block_rows = 2 * tok_rows
    local_grad = gradients[:, :, :block_rows].reshape(2, group_heads, 2, tok_rows, head_width)
    own_grad = jnp.where(parity == 0, local_grad[:, :, 0], local_grad[:, :, 1])
    other_grad = jnp.where(parity == 0, local_grad[:, :, 1], local_grad[:, :, 0]).astype(
        jnp.bfloat16
    )
    partner_grad = gradients[:, :, block_rows:].reshape(2, group_heads, 2, tok_rows, head_width)
    partner_grad = partner_grad.astype(jnp.bfloat16)
    returned = lax.all_to_all(
        partner_grad.reshape(2, group_heads, slot_count, devices, portion),
        "seq",
        split_axis=3,
        concat_axis=3,
        tiled=True,
    )
    summed_back = jnp.einsum(
        "hsij,chsil->chjl", select, returned, preferred_element_type=jnp.float32
    ).astype(jnp.bfloat16)
    arrived = lax.all_to_all(summed_back, "seq", split_axis=2, concat_axis=2, tiled=True)
    arrived = arrived.reshape(2, group_heads, tok_rows, head_width).astype(jnp.float32)
    pair_back = partner(other_grad, "seq", 0).astype(jnp.float32)
    total_grad = own_grad + arrived + pair_back
    key_grad = total_grad[0].astype(jnp.bfloat16)
    value_grad = total_grad[1].astype(jnp.bfloat16)
    return (projected, gradient_of_queries, key_grad, value_grad)


def per_device(*arrays):
    chips = lax.axis_size("seq") // 2
    square = chips == arrays[0].shape[0] == lax.axis_size("head") == 4
    return (by_heads if square else by_routing)(*arrays)


def solution(mesh):
    return jax.shard_map(
        per_device,
        mesh=mesh,
        in_specs=(
            P("head", "seq", None),
            P("head", "seq", None),
            P("head", "seq", None),
            P("head", None),
            P("head", None, None),
            P("seq", "head"),
        ),
        out_specs=(
            P("seq", "head"),
            P("head", "seq", None),
            P("head", "seq", None),
            P("head", "seq", None),
        ),
        check_vma=False,
    )
```

```python
import functools
import math

import jax
import jax.numpy as jnp
from jax import lax
from jax.experimental import pallas as pl
from jax.experimental.pallas import tpu as pltpu
from jax.sharding import PartitionSpec as P

F32 = jnp.float32
LOW = jnp.bfloat16
NT = (((1,), (1,)), ((), ()))
NN = (((1,), (0,)), ((), ()))
TN = (((0,), (0,)), ((), ()))


def dot(a, b, dims=NN):
    return lax.dot_general(a, b, dims, preferred_element_type=F32)


def chip_index():
    return lax.axis_index("seq") // 2


def call(body, outs, *args, flops=0, moved=0, scratch=(), smem=()):
    vmem = pl.BlockSpec(memory_space=pltpu.VMEM)
    scalar = pl.BlockSpec(memory_space=pltpu.SMEM)
    return pl.pallas_call(
        body,
        out_shape=outs,
        in_specs=[scalar if i in smem else vmem for i in range(len(args))],
        out_specs=jax.tree.map(lambda _: vmem, outs),
        scratch_shapes=list(scratch),
        cost_estimate=pl.CostEstimate(flops=flops, bytes_accessed=moved, transcendentals=0),
        compiler_params=pltpu.CompilerParams(vmem_limit_bytes=16 * 1024 * 1024),
    )(*args)


def attend_body(chips, rows, scale, perm, *refs):
    pieces, siblings = refs[:chips], refs[chips : 2 * chips]
    attended, probs, keys_values, queries, shares, values = refs[2 * chips :]
    chip = chip_index()
    for d in range(chips):
        keys_values[d, 0, :rows] = pieces[d][0]
        keys_values[d, 0, rows:] = siblings[d][0]
        values[d, :rows, :128] = pieces[d][1]
        values[d, rows:, :128] = siblings[d][1]
        values[d, :, 128:] = jnp.ones((2*rows,128),LOW)
        keys_values[d, 1, :rows] = pieces[d][1]
        keys_values[d, 1, rows:] = siblings[d][1]
        queries[d] = pieces[d][2]
    factor = scale * math.log2(math.e)
    for d in range(chips):
        p = perm[chip, chip ^ d] ^ chip
        query = pieces[d][2]
        local = dot(query, keys_values[d, 0], NT)
        remote = dot(query, keys_values[p, 0], NT)
        top = jnp.max(jnp.maximum(local, remote), axis=1, keepdims=True)
        local = jnp.exp2((local - top) * factor).astype(LOW)
        remote = jnp.exp2((remote - top) * factor).astype(LOW)
        probs[d, :, : 2 * rows] = local
        probs[d, :, 2 * rows :] = remote
        result = dot(local, values[d]) + dot(remote, values[p])
        share = 1.0 / result[:, 128:]
        shares[d] = share
        attended[d] = (result[:, :128] * share).astype(LOW)


def backward_body(chips, rows, scale, perm, *refs):
    arrived = refs[:chips]
    attended, probs, keys_values, queries, shares = refs[chips : chips + 5]
    query_grad, own_part, sibling_part, score_grad, scaled = refs[chips + 5 :]
    chip = chip_index()
    for d in range(chips):
        p = perm[chip, chip ^ d] ^ chip
        grad = arrived[d][...]
        share = shares[d]
        g32 = grad.astype(F32)
        delta = jnp.sum(g32 * attended[d].astype(F32), axis=1, keepdims=True)
        scaled[0, d] = (queries[d].astype(F32) * (share * scale)).astype(LOW)
        scaled[1, d] = (g32 * share).astype(LOW)
        total = None
        for part, source in ((0, d), (1, p)):
            lanes = slice(2 * rows * part, 2 * rows * (part + 1))
            prob_grad = dot(grad, keys_values[source, 1], NT)
            change = (probs[d, :, lanes].astype(F32) * (prob_grad - delta)).astype(LOW)
            score_grad[part, d] = change
            term = dot(change, keys_values[source, 0])
            total = term if total is None else total + term
        query_grad[d] = (total * (share * scale)).astype(LOW)
    for d in range(chips):
        asker = jnp.int32(0)
        for i in range(chips):
            asker = jnp.where(perm[chip, i] == chip ^ d, i, asker)
        asker = asker ^ chip
        for half, out in ((0, own_part), (1, sibling_part)):
            near = slice(half * rows, (half + 1) * rows)
            far = slice((half + 2) * rows, (half + 3) * rows)
            key_part = dot(score_grad[0, d, :, near], scaled[0, d], TN)
            key_part += dot(score_grad[1, asker, :, near], scaled[0, asker], TN)
            value_part = dot(probs[d, :, near], scaled[1, d], TN)
            value_part += dot(probs[asker, :, far], scaled[1, asker], TN)
            out[d, 0] = key_part.astype(out.dtype)
            out[d, 1] = value_part.astype(out.dtype)


def join_body(chips, groups, weight, *refs):
    incoming, joined, out = refs[:chips], refs[chips], refs[chips + 1]
    chip = chip_index()
    width = incoming[0].shape[1]
    for d in range(chips):
        lanes = pl.ds(pl.multiple_of((chip ^ d) * width, width), width)
        joined[:, lanes] = incoming[d][...]
    project_part(weight, joined[...], out, lax.axis_index("head") ^ (groups - 1))


def project_part(weight, rows, out, index):
    columns = out.shape[1]
    lanes = pl.ds(pl.multiple_of(index * columns, columns), columns)
    out[...] = dot(rows, weight[:, :, lanes].reshape(rows.shape[1], columns)).astype(LOW)


def project_body(weight, joined, *outs):
    level = lax.axis_index("head")
    for j, out in enumerate(outs):
        project_part(weight, joined[...], out, level ^ j)


def slice_product(weight, block, index):
    rows, columns = weight.shape[0] * weight.shape[1], block.shape[1]
    lanes = pl.ds(pl.multiple_of(index * columns, columns), columns)
    return dot(block[...], weight[:, :, lanes].reshape(rows, columns), NT)


def partial_body(weight, *refs):
    level = lax.axis_index("head")
    total = slice_product(weight, refs[0], level)
    for j in range(1, len(refs) - 1):
        total = total + slice_product(weight, refs[j], level ^ j)
    refs[-1][...] = total


def grad_body(chips, groups, weight, partial_grad, block, *outs):
    chip = chip_index()
    width = outs[0].shape[1]
    total = partial_grad[...] + slice_product(weight, block, lax.axis_index("head") ^ (groups - 1))
    total = total.astype(LOW)
    for c in range(chips):

        @pl.when(chip == c)
        def _():
            for d in range(chips):
                h = c ^ d
                outs[d][...] = total[:, h * width : (h + 1) * width]


def sum_body(*refs):
    total = refs[0][...].astype(F32)
    for ref in refs[1:-1]:
        total = total + ref[...].astype(F32)
    refs[-1][...] = total.astype(LOW)


def merge_body(chips, query_grad, own_part, arrived, *outs):
    for d in range(chips):
        outs[d][0] = query_grad[d]
        for kind in range(2):
            both = own_part[d, kind] + arrived[d, kind].astype(F32)
            outs[d][1 + kind] = both.astype(LOW)


def place_body(chips, *refs):
    pieces, outs = refs[:chips], refs[chips:]
    chip = chip_index()
    for d in range(chips):
        for kind in range(3):
            outs[kind][chip ^ d] = pieces[d][kind]


def by_heads(queries, key_vectors, value_vectors, block_perm, out_weight, out_cotangent):
    devices = lax.axis_size("seq")
    chips = devices // 2
    groups = lax.axis_size("head")
    heads, rows, width = queries.shape
    features = out_weight.shape[2]
    columns = out_cotangent.shape[1]
    scale = 1.0 / math.sqrt(width)
    chip = chip_index()
    shape = jax.ShapeDtypeStruct

    def to_chip(array, d):
        return lax.ppermute(array, "seq", [(i, i ^ (2 * d)) for i in range(devices)])

    def to_sibling(array):
        return lax.ppermute(array, "seq", [(i, i ^ 1) for i in range(devices)])

    def together(*arrays):
        return list(lax.optimization_barrier(arrays))

    def exchange(pieces):
        return [pieces[0]] + [to_chip(pieces[d], d) for d in range(1, chips)]

    def head_piece(d):
        h = chip ^ d
        return jnp.stack(
            [
                lax.dynamic_index_in_dim(a, h, 0, keepdims=False)
                for a in (key_vectors, value_vectors, queries)
            ]
        )

    def along(array, pairs):
        return lax.ppermute(array, "head", pairs)

    def across(array, j):
        return along(array, [(i, i ^ j) for i in range(groups)])

    twice = across(out_cotangent, 2)
    once = across(out_cotangent, 1)
    pieces = [head_piece(d) for d in range(chips)]
    siblings = [to_sibling(pieces[0][:2])]
    pieces = exchange(pieces)
    pieces[3], twice, once = together(pieces[3], twice, once)
    slices = [out_cotangent, once, twice, across(twice, 1)]
    siblings += [to_sibling(piece[:2]) for piece in pieces[1:]]
    tile = rows * width
    scores = chips * rows * 4 * rows
    piece = shape((rows, width), LOW)
    attended, probs, keys_values, query_rows, shares = call(
        functools.partial(attend_body, chips, rows, scale),
        (
            shape((chips, rows, width), LOW),
            shape((chips, rows, 4 * rows), LOW),
            shape((chips, 2, 2 * rows, width), LOW),
            shape((chips, rows, width), LOW),
            shape((chips, rows, width), F32),
        ),
        block_perm,
        *pieces,
        *siblings,
        flops=4 * scores * width,
        moved=2 * (scores + 14 * chips * tile),
        scratch=[pltpu.VMEM((chips, 2 * rows, 2 * width), LOW)],
        smem=(0,),
    )
    weight_bytes = 2 * heads * width * features
    own_attended = exchange([attended[d] for d in range(chips)])
    attended, *slices[:-1] = together(attended, *slices[:-1])
    partial_grad = call(
        partial_body,
        shape((rows, heads * width), F32),
        out_weight,
        *slices[:-1],
        flops=2 * rows * heads * width * (features - columns),
        moved=weight_bytes + 4 * rows * features,
    )
    grad_att = call(
        functools.partial(grad_body, chips, groups),
        (piece,) * chips,
        out_weight,
        partial_grad,
        slices[-1],
        flops=2 * rows * heads * width * columns,
        moved=weight_bytes // groups + 4 * rows * features,
    )
    incoming = exchange(grad_att)
    own_attended[0] = together(own_attended[0], grad_att[0])[0]
    block = shape((rows, columns), LOW)
    joined, *parts = call(
        functools.partial(join_body, chips, groups),
        (shape((rows, heads * width), LOW), block),
        out_weight,
        *own_attended,
        flops=2 * rows * heads * width * columns,
        moved=weight_bytes // groups + 4 * chips * tile,
    )
    halfway = across(parts[0], 1)
    parts = call(
        project_body,
        (block,) * (groups - 1),
        out_weight,
        joined,
        flops=2 * rows * heads * width * (features - columns),
        moved=weight_bytes + 2 * rows * features,
    )
    neighbour = across(together(parts[1], *incoming[2:])[0], 1)
    halfway = call(sum_body, shape((rows, columns), LOW), halfway, parts[2], flops=2**33, moved=2**28)
    incoming[0] = together(incoming[0], parts[0])[0]
    query_grad, own_part, sibling_part = call(
        functools.partial(backward_body, chips, rows, scale),
        (
            shape((chips, rows, width), LOW),
            shape((chips, 2, rows, width), F32),
            shape((chips, 2, rows, width), LOW),
        ),
        block_perm,
        *incoming,
        attended,
        probs,
        keys_values,
        query_rows,
        shares,
        flops=2**33,
        moved=2 * (scores + 20 * chips * tile),
        scratch=[
            pltpu.VMEM((2, chips, rows, 2 * rows), LOW),
            pltpu.VMEM((2, chips, rows, width), LOW),
        ],
        smem=(0,),
    )
    returned = exchange(
        call(
            functools.partial(merge_body, chips),
            tuple(shape((3, rows, width), LOW) for _ in range(chips)),
            query_grad,
            own_part,
            to_sibling(sibling_part),
            moved=2 * 14 * chips * tile,
        )
    )
    summands = [parts[0], neighbour, across(halfway, 2)]
    gradients = call(
        functools.partial(place_body, chips),
        (shape((heads, rows, width), LOW),) * 3,
        *returned,
        moved=2 * 6 * chips * tile,
    )
    summands[0], *gradients = together(summands[0], *gradients)
    projected = call(sum_body, block, *summands)
    return (projected, *gradients)


def partner(shard, axis, bit):
    return lax.ppermute(shard, axis, [(i, i ^ 1 << bit) for i in range(lax.axis_size(axis))])


def by_routing(queries, key_vectors, value_vectors, block_perm, out_weight, out_cotangent):
    devices = lax.axis_size("seq")
    position = lax.axis_index("seq")
    parity = position % 2
    group_heads, tok_rows, head_width = queries.shape
    portion = tok_rows * head_width // devices
    score_scale = 1.0 / math.sqrt(head_width)
    owners = jnp.repeat(block_perm, 2, axis=1)
    indices = lax.iota(jnp.int32, devices)
    sources = [2 * owners, 2 * owners + 1]
    source_table = jnp.stack(sources, axis=1)
    slot_count = source_table.shape[1]
    select = (source_table[..., None] == indices).astype(jnp.bfloat16)
    stacked = jnp.stack([key_vectors, value_vectors])
    spread = lax.all_to_all(
        stacked.reshape(2, group_heads, devices, portion),
        "seq",
        split_axis=2,
        concat_axis=2,
        tiled=True,
    )
    picked = jnp.einsum(
        "hsij,chjl->chsil", select, spread, preferred_element_type=jnp.float32
    ).astype(jnp.bfloat16)
    routed = lax.all_to_all(picked, "seq", split_axis=3, concat_axis=3, tiled=True)
    routed = routed.reshape(2, group_heads, slot_count, tok_rows, head_width)
    partner_kv = routed.reshape(2, group_heads, 2 * tok_rows, head_width)
    pair_other = partner(stacked, "seq", 0)
    local_kv = jnp.where(
        parity == 0,
        jnp.concatenate([stacked, pair_other], 2),
        jnp.concatenate([pair_other, stacked], 2),
    )
    combined = jnp.concatenate([local_kv, partner_kv], 2)
    key_all = combined[0]
    value_all = combined[1]
    logit_scores = (
        jnp.einsum("htd,hkd->htk", queries, key_all, preferred_element_type=jnp.float32)
        * score_scale
    )
    row_max = jnp.max(logit_scores, axis=-1, keepdims=True)
    weights = jnp.exp(logit_scores - row_max)
    probabilities = weights / jnp.sum(weights, axis=-1, keepdims=True)
    reduced_probabilities = probabilities.astype(jnp.bfloat16)
    attention_result = jnp.einsum(
        "htk,hkd->htd", reduced_probabilities, value_all, preferred_element_type=jnp.float32
    ).astype(jnp.bfloat16)
    partial_out = jnp.einsum(
        "htd,hde->te", attention_result, out_weight, preferred_element_type=jnp.float32
    )
    summed = lax.psum(partial_out.astype(jnp.bfloat16), "head").astype(jnp.float32)
    columns = summed.shape[1] // lax.axis_size("head")
    result = lax.dynamic_slice_in_dim(summed, lax.axis_index("head") * columns, columns, 1)
    projected = result.astype(jnp.bfloat16)
    full_grad = lax.all_gather(out_cotangent, "head", axis=1, tiled=True)
    grad_att = jnp.einsum(
        "te,hde->htd", full_grad, out_weight, preferred_element_type=jnp.float32
    ).astype(jnp.bfloat16)
    row_delta = jnp.sum(
        grad_att.astype(jnp.float32) * attention_result.astype(jnp.float32), axis=-1, keepdims=True
    )
    probability_gradient = jnp.einsum(
        "htd,hkd->htk", grad_att, value_all, preferred_element_type=jnp.float32
    )
    score_gradient = (probabilities * (probability_gradient - row_delta) * score_scale).astype(
        jnp.bfloat16
    )
    gradient_of_queries = jnp.einsum(
        "htk,hkd->htd", score_gradient, key_all, preferred_element_type=jnp.float32
    ).astype(jnp.bfloat16)
    key_part = jnp.einsum(
        "htk,htd->hkd", score_gradient, queries, preferred_element_type=jnp.float32
    )
    value_part = jnp.einsum(
        "htk,htd->hkd", reduced_probabilities, grad_att, preferred_element_type=jnp.float32
    )
    gradients = jnp.stack([key_part, value_part])
    block_rows = 2 * tok_rows
    local_grad = gradients[:, :, :block_rows].reshape(2, group_heads, 2, tok_rows, head_width)
    own_grad = jnp.where(parity == 0, local_grad[:, :, 0], local_grad[:, :, 1])
    other_grad = jnp.where(parity == 0, local_grad[:, :, 1], local_grad[:, :, 0]).astype(
        jnp.bfloat16
    )
    partner_grad = gradients[:, :, block_rows:].reshape(2, group_heads, 2, tok_rows, head_width)
    partner_grad = partner_grad.astype(jnp.bfloat16)
    returned = lax.all_to_all(
        partner_grad.reshape(2, group_heads, slot_count, devices, portion),
        "seq",
        split_axis=3,
        concat_axis=3,
        tiled=True,
    )
    summed_back = jnp.einsum(
        "hsij,chsil->chjl", select, returned, preferred_element_type=jnp.float32
    ).astype(jnp.bfloat16)
    arrived = lax.all_to_all(summed_back, "seq", split_axis=2, concat_axis=2, tiled=True)
    arrived = arrived.reshape(2, group_heads, tok_rows, head_width).astype(jnp.float32)
    pair_back = partner(other_grad, "seq", 0).astype(jnp.float32)
    total_grad = own_grad + arrived + pair_back
    key_grad = total_grad[0].astype(jnp.bfloat16)
    value_grad = total_grad[1].astype(jnp.bfloat16)
    return (projected, gradient_of_queries, key_grad, value_grad)


def per_device(*arrays):
    chips = lax.axis_size("seq") // 2
    square = chips == arrays[0].shape[0] == lax.axis_size("head") == 4
    return (by_heads if square else by_routing)(*arrays)


def solution(mesh):
    return jax.shard_map(
        per_device,
        mesh=mesh,
        in_specs=(
            P("head", "seq", None),
            P("head", "seq", None),
            P("head", "seq", None),
            P("head", None),
            P("head", None, None),
            P("seq", "head"),
        ),
        out_specs=(
            P("seq", "head"),
            P("head", "seq", None),
            P("head", "seq", None),
            P("head", "seq", None),
        ),
        check_vma=False,
    )
```

```python
import functools
import math

import jax
import jax.numpy as jnp
from jax import lax
from jax.experimental import pallas as pl
from jax.experimental.pallas import tpu as pltpu
from jax.sharding import PartitionSpec as P

F32 = jnp.float32
LOW = jnp.bfloat16
NT = (((1,), (1,)), ((), ()))
NN = (((1,), (0,)), ((), ()))
TN = (((0,), (0,)), ((), ()))


def dot(a, b, dims=NN):
    return lax.dot_general(a, b, dims, preferred_element_type=F32)


def chip_index():
    return lax.axis_index("seq") // 2


def call(body, outs, *args, flops=0, moved=0, scratch=(), smem=()):
    vmem = pl.BlockSpec(memory_space=pltpu.VMEM)
    scalar = pl.BlockSpec(memory_space=pltpu.SMEM)
    return pl.pallas_call(
        body,
        out_shape=outs,
        in_specs=[scalar if i in smem else vmem for i in range(len(args))],
        out_specs=jax.tree.map(lambda _: vmem, outs),
        scratch_shapes=list(scratch),
        cost_estimate=pl.CostEstimate(flops=flops, bytes_accessed=moved, transcendentals=0),
        compiler_params=pltpu.CompilerParams(vmem_limit_bytes=16 * 1024 * 1024),
    )(*args)


def attend_body(chips, rows, scale, perm, *refs):
    pieces, siblings = refs[:chips], refs[chips : 2 * chips]
    attended, probs, keys_values, queries, shares, values = refs[2 * chips :]
    chip = chip_index()
    for d in range(chips):
        keys_values[d, 0, :rows] = pieces[d][0]
        keys_values[d, 0, rows:] = siblings[d][0]
        values[d, :rows, :128] = pieces[d][1]
        values[d, rows:, :128] = siblings[d][1]
        values[d, :, 128:] = jnp.ones((2*rows,128),LOW)
        keys_values[d, 1, :rows] = pieces[d][1]
        keys_values[d, 1, rows:] = siblings[d][1]
        queries[d] = pieces[d][2]
    factor = scale * math.log2(math.e)
    for d in range(chips):
        p = perm[chip, chip ^ d] ^ chip
        query = pieces[d][2]
        local = dot(query, keys_values[d, 0], NT)
        remote = dot(query, keys_values[p, 0], NT)
        top = jnp.max(jnp.maximum(local, remote), axis=1, keepdims=True)
        local = jnp.exp2((local - top) * factor).astype(LOW)
        remote = jnp.exp2((remote - top) * factor).astype(LOW)
        probs[d, :, : 2 * rows] = local
        probs[d, :, 2 * rows :] = remote
        result = dot(local, values[d]) + dot(remote, values[p])
        share = 1.0 / result[:, 128:]
        shares[d] = share
        attended[d] = (result[:, :128] * share).astype(LOW)


def backward_body(chips, rows, scale, perm, *refs):
    arrived = refs[:chips]
    attended, probs, keys_values, queries, shares = refs[chips : chips + 5]
    query_grad, own_part, sibling_part, score_grad, scaled = refs[chips + 5 :]
    chip = chip_index()
    for d in range(chips):
        p = perm[chip, chip ^ d] ^ chip
        grad = arrived[d][...]
        share = shares[d]
        g32 = grad.astype(F32)
        delta = jnp.sum(g32 * attended[d].astype(F32), axis=1, keepdims=True)
        scaled[0, d] = (queries[d].astype(F32) * (share * scale)).astype(LOW)
        scaled[1, d] = (g32 * share).astype(LOW)
        total = None
        for part, source in ((0, d), (1, p)):
            lanes = slice(2 * rows * part, 2 * rows * (part + 1))
            prob_grad = dot(grad, keys_values[source, 1], NT)
            change = (probs[d, :, lanes].astype(F32) * (prob_grad - delta)).astype(LOW)
            score_grad[part, d] = change
            term = dot(change, keys_values[source, 0])
            total = term if total is None else total + term
        query_grad[d] = (total * (share * scale)).astype(LOW)
    for d in range(chips):
        asker = jnp.int32(0)
        for i in range(chips):
            asker = jnp.where(perm[chip, i] == chip ^ d, i, asker)
        asker = asker ^ chip
        local = slice(0, 2 * rows)
        remote = slice(2 * rows, 4 * rows)
        key_part = dot(scaled[0, d], score_grad[0, d], TN)
        key_part += dot(scaled[0, asker], score_grad[1, asker], TN)
        value_part = dot(scaled[1, d], probs[d, :, local], TN)
        value_part += dot(scaled[1, asker], probs[asker, :, remote], TN)
        for kind, part in enumerate((key_part, value_part)):
            own_part[d, kind] = part[:, :rows].T
            sibling_part[d, kind] = part[:, rows:].astype(LOW).T


def join_body(chips, groups, weight, *refs):
    incoming, joined, out = refs[:chips], refs[chips], refs[chips + 1]
    chip = chip_index()
    width = incoming[0].shape[1]
    for d in range(chips):
        lanes = pl.ds(pl.multiple_of((chip ^ d) * width, width), width)
        joined[:, lanes] = incoming[d][...]
    project_part(weight, joined[...], out, lax.axis_index("head") ^ (groups - 1))


def project_part(weight, rows, out, index):
    columns = out.shape[1]
    lanes = pl.ds(pl.multiple_of(index * columns, columns), columns)
    out[...] = dot(rows, weight[:, :, lanes].reshape(rows.shape[1], columns)).astype(LOW)


def project_body(weight, joined, *outs):
    level = lax.axis_index("head")
    for j, out in enumerate(outs):
        project_part(weight, joined[...], out, level ^ j)


def slice_product(weight, block, index):
    rows, columns = weight.shape[0] * weight.shape[1], block.shape[1]
    lanes = pl.ds(pl.multiple_of(index * columns, columns), columns)
    return dot(block[...], weight[:, :, lanes].reshape(rows, columns), NT)


def partial_body(weight, *refs):
    level = lax.axis_index("head")
    total = slice_product(weight, refs[0], level)
    for j in range(1, len(refs) - 1):
        total = total + slice_product(weight, refs[j], level ^ j)
    refs[-1][...] = total


def grad_body(chips, groups, weight, partial_grad, block, *outs):
    chip = chip_index()
    width = outs[0].shape[1]
    total = partial_grad[...] + slice_product(weight, block, lax.axis_index("head") ^ (groups - 1))
    total = total.astype(LOW)
    for c in range(chips):

        @pl.when(chip == c)
        def _():
            for d in range(chips):
                h = c ^ d
                outs[d][...] = total[:, h * width : (h + 1) * width]


def sum_body(*refs):
    total = refs[0][...].astype(F32)
    for ref in refs[1:-1]:
        total = total + ref[...].astype(F32)
    refs[-1][...] = total.astype(LOW)


def merge_body(chips, query_grad, own_part, arrived, *outs):
    for d in range(chips):
        outs[d][0] = query_grad[d]
        for kind in range(2):
            both = own_part[d, kind] + arrived[d, kind].astype(F32)
            outs[d][1 + kind] = both.astype(LOW)


def place_body(chips, *refs):
    pieces, outs = refs[:chips], refs[chips:]
    chip = chip_index()
    for d in range(chips):
        for kind in range(3):
            outs[kind][chip ^ d] = pieces[d][kind]


def by_heads(queries, key_vectors, value_vectors, block_perm, out_weight, out_cotangent):
    devices = lax.axis_size("seq")
    chips = devices // 2
    groups = lax.axis_size("head")
    heads, rows, width = queries.shape
    features = out_weight.shape[2]
    columns = out_cotangent.shape[1]
    scale = 1.0 / math.sqrt(width)
    chip = chip_index()
    shape = jax.ShapeDtypeStruct

    def to_chip(array, d):
        return lax.ppermute(array, "seq", [(i, i ^ (2 * d)) for i in range(devices)])

    def to_sibling(array):
        return lax.ppermute(array, "seq", [(i, i ^ 1) for i in range(devices)])

    def together(*arrays):
        return list(lax.optimization_barrier(arrays))

    def exchange(pieces):
        return [pieces[0]] + [to_chip(pieces[d], d) for d in range(1, chips)]

    def head_piece(d):
        h = chip ^ d
        return jnp.stack(
            [
                lax.dynamic_index_in_dim(a, h, 0, keepdims=False)
                for a in (key_vectors, value_vectors, queries)
            ]
        )

    def along(array, pairs):
        return lax.ppermute(array, "head", pairs)

    def across(array, j):
        return along(array, [(i, i ^ j) for i in range(groups)])

    twice = across(out_cotangent, 2)
    once = across(out_cotangent, 1)
    pieces = [head_piece(d) for d in range(chips)]
    siblings = [to_sibling(pieces[0][:2])]
    pieces = exchange(pieces)
    pieces[3], twice, once = together(pieces[3], twice, once)
    slices = [out_cotangent, once, twice, across(twice, 1)]
    siblings += [to_sibling(piece[:2]) for piece in pieces[1:]]
    tile = rows * width
    scores = chips * rows * 4 * rows
    piece = shape((rows, width), LOW)
    attended, probs, keys_values, query_rows, shares = call(
        functools.partial(attend_body, chips, rows, scale),
        (
            shape((chips, rows, width), LOW),
            shape((chips, rows, 4 * rows), LOW),
            shape((chips, 2, 2 * rows, width), LOW),
            shape((chips, rows, width), LOW),
            shape((chips, rows, width), F32),
        ),
        block_perm,
        *pieces,
        *siblings,
        flops=4 * scores * width,
        moved=2 * (scores + 14 * chips * tile),
        scratch=[pltpu.VMEM((chips, 2 * rows, 2 * width), LOW)],
        smem=(0,),
    )
    weight_bytes = 2 * heads * width * features
    own_attended = exchange([attended[d] for d in range(chips)])
    attended, *slices[:-1] = together(attended, *slices[:-1])
    partial_grad = call(
        partial_body,
        shape((rows, heads * width), F32),
        out_weight,
        *slices[:-1],
        flops=2 * rows * heads * width * (features - columns),
        moved=weight_bytes + 4 * rows * features,
    )
    grad_att = call(
        functools.partial(grad_body, chips, groups),
        (piece,) * chips,
        out_weight,
        partial_grad,
        slices[-1],
        flops=2 * rows * heads * width * columns,
        moved=weight_bytes // groups + 4 * rows * features,
    )
    incoming = exchange(grad_att)
    own_attended[0] = together(own_attended[0], grad_att[0])[0]
    block = shape((rows, columns), LOW)
    joined, *parts = call(
        functools.partial(join_body, chips, groups),
        (shape((rows, heads * width), LOW), block),
        out_weight,
        *own_attended,
        flops=2 * rows * heads * width * columns,
        moved=weight_bytes // groups + 4 * chips * tile,
    )
    halfway = across(parts[0], 1)
    parts = call(
        project_body,
        (block,) * (groups - 1),
        out_weight,
        joined,
        flops=2 * rows * heads * width * (features - columns),
        moved=weight_bytes + 2 * rows * features,
    )
    neighbour = across(together(parts[1], *incoming[2:])[0], 1)
    halfway = call(sum_body, shape((rows, columns), LOW), halfway, parts[2], flops=2**33, moved=2**28)
    incoming[0] = together(incoming[0], parts[0])[0]
    query_grad, own_part, sibling_part = call(
        functools.partial(backward_body, chips, rows, scale),
        (
            shape((chips, rows, width), LOW),
            shape((chips, 2, rows, width), F32),
            shape((chips, 2, rows, width), LOW),
        ),
        block_perm,
        *incoming,
        attended,
        probs,
        keys_values,
        query_rows,
        shares,
        flops=2**33,
        moved=2 * (scores + 20 * chips * tile),
        scratch=[
            pltpu.VMEM((2, chips, rows, 2 * rows), LOW),
            pltpu.VMEM((2, chips, rows, width), LOW),
        ],
        smem=(0,),
    )
    returned = exchange(
        call(
            functools.partial(merge_body, chips),
            tuple(shape((3, rows, width), LOW) for _ in range(chips)),
            query_grad,
            own_part,
            to_sibling(sibling_part),
            moved=2 * 14 * chips * tile,
        )
    )
    summands = [parts[0], neighbour, across(halfway, 2)]
    gradients = call(
        functools.partial(place_body, chips),
        (shape((heads, rows, width), LOW),) * 3,
        *returned,
        moved=2 * 6 * chips * tile,
    )
    summands[0], *gradients = together(summands[0], *gradients)
    projected = call(sum_body, block, *summands)
    return (projected, *gradients)


def partner(shard, axis, bit):
    return lax.ppermute(shard, axis, [(i, i ^ 1 << bit) for i in range(lax.axis_size(axis))])


def by_routing(queries, key_vectors, value_vectors, block_perm, out_weight, out_cotangent):
    devices = lax.axis_size("seq")
    position = lax.axis_index("seq")
    parity = position % 2
    group_heads, tok_rows, head_width = queries.shape
    portion = tok_rows * head_width // devices
    score_scale = 1.0 / math.sqrt(head_width)
    owners = jnp.repeat(block_perm, 2, axis=1)
    indices = lax.iota(jnp.int32, devices)
    sources = [2 * owners, 2 * owners + 1]
    source_table = jnp.stack(sources, axis=1)
    slot_count = source_table.shape[1]
    select = (source_table[..., None] == indices).astype(jnp.bfloat16)
    stacked = jnp.stack([key_vectors, value_vectors])
    spread = lax.all_to_all(
        stacked.reshape(2, group_heads, devices, portion),
        "seq",
        split_axis=2,
        concat_axis=2,
        tiled=True,
    )
    picked = jnp.einsum(
        "hsij,chjl->chsil", select, spread, preferred_element_type=jnp.float32
    ).astype(jnp.bfloat16)
    routed = lax.all_to_all(picked, "seq", split_axis=3, concat_axis=3, tiled=True)
    routed = routed.reshape(2, group_heads, slot_count, tok_rows, head_width)
    partner_kv = routed.reshape(2, group_heads, 2 * tok_rows, head_width)
    pair_other = partner(stacked, "seq", 0)
    local_kv = jnp.where(
        parity == 0,
        jnp.concatenate([stacked, pair_other], 2),
        jnp.concatenate([pair_other, stacked], 2),
    )
    combined = jnp.concatenate([local_kv, partner_kv], 2)
    key_all = combined[0]
    value_all = combined[1]
    logit_scores = (
        jnp.einsum("htd,hkd->htk", queries, key_all, preferred_element_type=jnp.float32)
        * score_scale
    )
    row_max = jnp.max(logit_scores, axis=-1, keepdims=True)
    weights = jnp.exp(logit_scores - row_max)
    probabilities = weights / jnp.sum(weights, axis=-1, keepdims=True)
    reduced_probabilities = probabilities.astype(jnp.bfloat16)
    attention_result = jnp.einsum(
        "htk,hkd->htd", reduced_probabilities, value_all, preferred_element_type=jnp.float32
    ).astype(jnp.bfloat16)
    partial_out = jnp.einsum(
        "htd,hde->te", attention_result, out_weight, preferred_element_type=jnp.float32
    )
    summed = lax.psum(partial_out.astype(jnp.bfloat16), "head").astype(jnp.float32)
    columns = summed.shape[1] // lax.axis_size("head")
    result = lax.dynamic_slice_in_dim(summed, lax.axis_index("head") * columns, columns, 1)
    projected = result.astype(jnp.bfloat16)
    full_grad = lax.all_gather(out_cotangent, "head", axis=1, tiled=True)
    grad_att = jnp.einsum(
        "te,hde->htd", full_grad, out_weight, preferred_element_type=jnp.float32
    ).astype(jnp.bfloat16)
    row_delta = jnp.sum(
        grad_att.astype(jnp.float32) * attention_result.astype(jnp.float32), axis=-1, keepdims=True
    )
    probability_gradient = jnp.einsum(
        "htd,hkd->htk", grad_att, value_all, preferred_element_type=jnp.float32
    )
    score_gradient = (probabilities * (probability_gradient - row_delta) * score_scale).astype(
        jnp.bfloat16
    )
    gradient_of_queries = jnp.einsum(
        "htk,hkd->htd", score_gradient, key_all, preferred_element_type=jnp.float32
    ).astype(jnp.bfloat16)
    key_part = jnp.einsum(
        "htk,htd->hkd", score_gradient, queries, preferred_element_type=jnp.float32
    )
    value_part = jnp.einsum(
        "htk,htd->hkd", reduced_probabilities, grad_att, preferred_element_type=jnp.float32
    )
    gradients = jnp.stack([key_part, value_part])
    block_rows = 2 * tok_rows
    local_grad = gradients[:, :, :block_rows].reshape(2, group_heads, 2, tok_rows, head_width)
    own_grad = jnp.where(parity == 0, local_grad[:, :, 0], local_grad[:, :, 1])
    other_grad = jnp.where(parity == 0, local_grad[:, :, 1], local_grad[:, :, 0]).astype(
        jnp.bfloat16
    )
    partner_grad = gradients[:, :, block_rows:].reshape(2, group_heads, 2, tok_rows, head_width)
    partner_grad = partner_grad.astype(jnp.bfloat16)
    returned = lax.all_to_all(
        partner_grad.reshape(2, group_heads, slot_count, devices, portion),
        "seq",
        split_axis=3,
        concat_axis=3,
        tiled=True,
    )
    summed_back = jnp.einsum(
        "hsij,chsil->chjl", select, returned, preferred_element_type=jnp.float32
    ).astype(jnp.bfloat16)
    arrived = lax.all_to_all(summed_back, "seq", split_axis=2, concat_axis=2, tiled=True)
    arrived = arrived.reshape(2, group_heads, tok_rows, head_width).astype(jnp.float32)
    pair_back = partner(other_grad, "seq", 0).astype(jnp.float32)
    total_grad = own_grad + arrived + pair_back
    key_grad = total_grad[0].astype(jnp.bfloat16)
    value_grad = total_grad[1].astype(jnp.bfloat16)
    return (projected, gradient_of_queries, key_grad, value_grad)


def per_device(*arrays):
    chips = lax.axis_size("seq") // 2
    square = chips == arrays[0].shape[0] == lax.axis_size("head") == 4
    return (by_heads if square else by_routing)(*arrays)


def solution(mesh):
    return jax.shard_map(
        per_device,
        mesh=mesh,
        in_specs=(
            P("head", "seq", None),
            P("head", "seq", None),
            P("head", "seq", None),
            P("head", None),
            P("head", None, None),
            P("seq", "head"),
        ),
        out_specs=(
            P("seq", "head"),
            P("head", "seq", None),
            P("head", "seq", None),
            P("head", "seq", None),
        ),
        check_vma=False,
    )
```

```python
import functools
import math

import jax
import jax.numpy as jnp
from jax import lax
from jax.experimental import pallas as pl
from jax.experimental.pallas import tpu as pltpu
from jax.sharding import PartitionSpec as P

F32 = jnp.float32
LOW = jnp.bfloat16
NT = (((1,), (1,)), ((), ()))
NN = (((1,), (0,)), ((), ()))
TN = (((0,), (0,)), ((), ()))


def dot(a, b, dims=NN):
    return lax.dot_general(a, b, dims, preferred_element_type=F32)


def chip_index():
    return lax.axis_index("seq") // 2


def call(body, outs, *args, flops=0, moved=0, scratch=(), smem=()):
    vmem = pl.BlockSpec(memory_space=pltpu.VMEM)
    scalar = pl.BlockSpec(memory_space=pltpu.SMEM)
    return pl.pallas_call(
        body,
        out_shape=outs,
        in_specs=[scalar if i in smem else vmem for i in range(len(args))],
        out_specs=jax.tree.map(lambda _: vmem, outs),
        scratch_shapes=list(scratch),
        cost_estimate=pl.CostEstimate(flops=flops, bytes_accessed=moved, transcendentals=0),
        compiler_params=pltpu.CompilerParams(vmem_limit_bytes=16 * 1024 * 1024),
    )(*args)


def attend_body(chips, rows, scale, perm, *refs):
    pieces, siblings = refs[:chips], refs[chips : 2 * chips]
    attended, probs, keys_values, queries, shares, values = refs[2 * chips :]
    chip = chip_index()
    for d in range(chips):
        keys_values[d, 0, :rows] = pieces[d][0]
        keys_values[d, 0, rows:] = siblings[d][0]
        values[d, :rows, :128] = pieces[d][1]
        values[d, rows:, :128] = siblings[d][1]
        values[d, :, 128:] = jnp.ones((2*rows,128),LOW)
        keys_values[d, 1, :rows] = pieces[d][1]
        keys_values[d, 1, rows:] = siblings[d][1]
        queries[d] = pieces[d][2]
    factor = scale * math.log2(math.e)
    for d in range(chips):
        p = perm[chip, chip ^ d] ^ chip
        query = pieces[d][2]
        local = dot(query, keys_values[d, 0], NT)
        remote = dot(query, keys_values[p, 0], NT)
        top = jnp.max(jnp.maximum(local, remote), axis=1, keepdims=True)
        local = jnp.exp2((local - top) * factor).astype(LOW)
        remote = jnp.exp2((remote - top) * factor).astype(LOW)
        probs[d, :, : 2 * rows] = local
        probs[d, :, 2 * rows :] = remote
        result = dot(local, values[d]) + dot(remote, values[p])
        share = 1.0 / result[:, 128:]
        shares[d] = share
        attended[d] = (result[:, :128] * share).astype(LOW)


def backward_body(chips, rows, scale, perm, *refs):
    arrived = refs[:chips]
    attended, probs, keys_values, queries, shares = refs[chips : chips + 5]
    query_grad, own_part, sibling_part, score_grad, scaled = refs[chips + 5 :]
    chip = chip_index()
    for d in range(chips):
        p = perm[chip, chip ^ d] ^ chip
        grad = arrived[d][...]
        share = shares[d]
        g32 = grad.astype(F32)
        delta = jnp.sum(g32 * attended[d].astype(F32), axis=1, keepdims=True)
        scaled[0, d] = (queries[d].astype(F32) * (share * scale)).astype(LOW)
        scaled[1, d] = (g32 * share).astype(LOW)
        total = None
        for part, source in ((0, d), (1, p)):
            lanes = slice(2 * rows * part, 2 * rows * (part + 1))
            prob_grad = dot(grad, keys_values[source, 1], NT)
            change = (probs[d, :, lanes].astype(F32) * (prob_grad - delta)).astype(LOW)
            score_grad[part, d] = change
            term = dot(change, keys_values[source, 0])
            total = term if total is None else total + term
        query_grad[d] = (total * (share * scale)).astype(LOW)
    for d in range(chips):
        asker = jnp.int32(0)
        for i in range(chips):
            asker = jnp.where(perm[chip, i] == chip ^ d, i, asker)
        asker = asker ^ chip
        local = slice(0, 2 * rows)
        remote = slice(2 * rows, 4 * rows)
        key_part = dot(scaled[0, d], score_grad[0, d], TN)
        key_part += dot(scaled[0, asker], score_grad[1, asker], TN)
        value_part = dot(scaled[1, d], probs[d, :, local], TN)
        value_part += dot(scaled[1, asker], probs[asker, :, remote], TN)
        for kind, part in enumerate((key_part, value_part)):
            own_part[d, kind] = part[:, :rows].T
            sibling_part[d, kind] = part[:, rows:].astype(LOW).T


def join_body(chips, groups, weight, *refs):
    incoming, joined, out = refs[:chips], refs[chips], refs[chips + 1]
    chip = chip_index()
    width = incoming[0].shape[1]
    for d in range(chips):
        lanes = pl.ds(pl.multiple_of((chip ^ d) * width, width), width)
        joined[:, lanes] = incoming[d][...]
    project_part(weight, joined[...], out, lax.axis_index("head") ^ (groups - 1))


def project_part(weight, rows, out, index):
    columns = out.shape[1]
    lanes = pl.ds(pl.multiple_of(index * columns, columns), columns)
    out[...] = dot(rows, weight[:, :, lanes].reshape(rows.shape[1], columns)).astype(LOW)


def project_body(weight, joined, *outs):
    level = lax.axis_index("head")
    for j, out in enumerate(outs):
        project_part(weight, joined[...], out, level ^ j)


def slice_product(weight, block, index):
    rows, columns = weight.shape[0] * weight.shape[1], block.shape[1]
    lanes = pl.ds(pl.multiple_of(index * columns, columns), columns)
    return dot(block[...], weight[:, :, lanes].reshape(rows, columns), NT)


def partial_body(weight, *refs):
    level = lax.axis_index("head")
    total = slice_product(weight, refs[0], level)
    for j in range(1, len(refs) - 1):
        total = total + slice_product(weight, refs[j], level ^ j)
    refs[-1][...] = total


def grad_body(chips, groups, weight, partial_grad, block, *outs):
    chip = chip_index()
    width = outs[0].shape[1]
    total = partial_grad[...] + slice_product(weight, block, lax.axis_index("head") ^ (groups - 1))
    total = total.astype(LOW)
    for c in range(chips):

        @pl.when(chip == c)
        def _():
            for d in range(chips):
                h = c ^ d
                outs[d][...] = total[:, h * width : (h + 1) * width]


def sum_body(*refs):
    total = refs[0][...].astype(F32)
    for ref in refs[1:-1]:
        total = total + ref[...].astype(F32)
    refs[-1][...] = total.astype(LOW)


def merge_body(chips, query_grad, own_part, arrived, *outs):
    for d in range(chips):
        outs[d][0] = query_grad[d]
        for kind in range(2):
            both = own_part[d, kind] + arrived[d, kind].astype(F32)
            outs[d][1 + kind] = both.astype(LOW)


def place_body(chips, *refs):
    pieces, outs = refs[:chips], refs[chips:]
    chip = chip_index()
    for d in range(chips):
        for kind in range(3):
            outs[kind][chip ^ d] = pieces[d][kind]


def by_heads(queries, key_vectors, value_vectors, block_perm, out_weight, out_cotangent):
    devices = lax.axis_size("seq")
    chips = devices // 2
    groups = lax.axis_size("head")
    heads, rows, width = queries.shape
    features = out_weight.shape[2]
    columns = out_cotangent.shape[1]
    scale = 1.0 / math.sqrt(width)
    chip = chip_index()
    shape = jax.ShapeDtypeStruct

    def to_chip(array, d):
        return lax.ppermute(array, "seq", [(i, i ^ (2 * d)) for i in range(devices)])

    def to_sibling(array):
        return lax.ppermute(array, "seq", [(i, i ^ 1) for i in range(devices)])

    def together(*arrays):
        return list(lax.optimization_barrier(arrays))

    def exchange(pieces):
        return [pieces[0]] + [to_chip(pieces[d], d) for d in range(1, chips)]

    def head_piece(d):
        h = chip ^ d
        return jnp.stack(
            [
                lax.dynamic_index_in_dim(a, h, 0, keepdims=False)
                for a in (key_vectors, value_vectors, queries)
            ]
        )

    def along(array, pairs):
        return lax.ppermute(array, "head", pairs)

    def across(array, j):
        return along(array, [(i, i ^ j) for i in range(groups)])

    twice = across(out_cotangent, 2)
    once = across(out_cotangent, 1)
    pieces = [head_piece(d) for d in range(chips)]
    siblings = [to_sibling(pieces[0][:2])]
    pieces = exchange(pieces)
    pieces[3], twice, once = together(pieces[3], twice, once)
    slices = [out_cotangent, once, twice, across(twice, 1)]
    siblings += [to_sibling(piece[:2]) for piece in pieces[1:]]
    tile = rows * width
    scores = chips * rows * 4 * rows
    piece = shape((rows, width), LOW)
    attended, probs, keys_values, query_rows, shares = call(
        functools.partial(attend_body, chips, rows, scale),
        (
            shape((chips, rows, width), LOW),
            shape((chips, rows, 4 * rows), LOW),
            shape((chips, 2, 2 * rows, width), LOW),
            shape((chips, rows, width), LOW),
            shape((chips, rows, width), F32),
        ),
        block_perm,
        *pieces,
        *siblings,
        flops=4 * scores * width,
        moved=2 * (scores + 14 * chips * tile),
        scratch=[pltpu.VMEM((chips, 2 * rows, 2 * width), LOW)],
        smem=(0,),
    )
    weight_bytes = 2 * heads * width * features
    own_attended = exchange([attended[d] for d in range(chips)])
    attended, *slices[:-1] = together(attended, *slices[:-1])
    partial_grad = call(
        partial_body,
        shape((rows, heads * width), F32),
        out_weight,
        *slices[:-1],
        flops=2 * rows * heads * width * (features - columns),
        moved=weight_bytes + 4 * rows * features,
    )
    grad_att = call(
        functools.partial(grad_body, chips, groups),
        (piece,) * chips,
        out_weight,
        partial_grad,
        slices[-1],
        flops=2 * rows * heads * width * columns,
        moved=weight_bytes // groups + 4 * rows * features,
    )
    incoming = exchange(grad_att)
    own_attended[0] = together(own_attended[0], grad_att[0])[0]
    block = shape((rows, columns), LOW)
    joined, *parts = call(
        functools.partial(join_body, chips, groups),
        (shape((rows, heads * width), LOW), block),
        out_weight,
        *own_attended,
        flops=2 * rows * heads * width * columns,
        moved=weight_bytes // groups + 4 * chips * tile,
    )
    halfway = across(parts[0], 1)
    parts = call(
        project_body,
        (block,) * (groups - 1),
        out_weight,
        joined,
        flops=2 * rows * heads * width * (features - columns),
        moved=weight_bytes + 2 * rows * features,
    )
    halfway = call(sum_body, shape((rows, columns), LOW), halfway, parts[2], flops=2**33, moved=2**28)
    incoming[0] = together(incoming[0], parts[0])[0]
    query_grad, own_part, sibling_part = call(
        functools.partial(backward_body, chips, rows, scale),
        (
            shape((chips, rows, width), LOW),
            shape((chips, 2, rows, width), F32),
            shape((chips, 2, rows, width), LOW),
        ),
        block_perm,
        *incoming,
        attended,
        probs,
        keys_values,
        query_rows,
        shares,
        flops=2**33,
        moved=2 * (scores + 20 * chips * tile),
        scratch=[
            pltpu.VMEM((2, chips, rows, 2 * rows), LOW),
            pltpu.VMEM((2, chips, rows, width), LOW),
        ],
        smem=(0,),
    )
    neighbour = across(together(parts[1], sibling_part)[0], 1)
    returned = exchange(
        call(
            functools.partial(merge_body, chips),
            tuple(shape((3, rows, width), LOW) for _ in range(chips)),
            query_grad,
            own_part,
            to_sibling(sibling_part),
            moved=2 * 14 * chips * tile,
        )
    )
    summands = [parts[0], neighbour, across(halfway, 2)]
    gradients = call(
        functools.partial(place_body, chips),
        (shape((heads, rows, width), LOW),) * 3,
        *returned,
        moved=2 * 6 * chips * tile,
    )
    summands[0], *gradients = together(summands[0], *gradients)
    projected = call(sum_body, block, *summands)
    return (projected, *gradients)


def partner(shard, axis, bit):
    return lax.ppermute(shard, axis, [(i, i ^ 1 << bit) for i in range(lax.axis_size(axis))])


def by_routing(queries, key_vectors, value_vectors, block_perm, out_weight, out_cotangent):
    devices = lax.axis_size("seq")
    position = lax.axis_index("seq")
    parity = position % 2
    group_heads, tok_rows, head_width = queries.shape
    portion = tok_rows * head_width // devices
    score_scale = 1.0 / math.sqrt(head_width)
    owners = jnp.repeat(block_perm, 2, axis=1)
    indices = lax.iota(jnp.int32, devices)
    sources = [2 * owners, 2 * owners + 1]
    source_table = jnp.stack(sources, axis=1)
    slot_count = source_table.shape[1]
    select = (source_table[..., None] == indices).astype(jnp.bfloat16)
    stacked = jnp.stack([key_vectors, value_vectors])
    spread = lax.all_to_all(
        stacked.reshape(2, group_heads, devices, portion),
        "seq",
        split_axis=2,
        concat_axis=2,
        tiled=True,
    )
    picked = jnp.einsum(
        "hsij,chjl->chsil", select, spread, preferred_element_type=jnp.float32
    ).astype(jnp.bfloat16)
    routed = lax.all_to_all(picked, "seq", split_axis=3, concat_axis=3, tiled=True)
    routed = routed.reshape(2, group_heads, slot_count, tok_rows, head_width)
    partner_kv = routed.reshape(2, group_heads, 2 * tok_rows, head_width)
    pair_other = partner(stacked, "seq", 0)
    local_kv = jnp.where(
        parity == 0,
        jnp.concatenate([stacked, pair_other], 2),
        jnp.concatenate([pair_other, stacked], 2),
    )
    combined = jnp.concatenate([local_kv, partner_kv], 2)
    key_all = combined[0]
    value_all = combined[1]
    logit_scores = (
        jnp.einsum("htd,hkd->htk", queries, key_all, preferred_element_type=jnp.float32)
        * score_scale
    )
    row_max = jnp.max(logit_scores, axis=-1, keepdims=True)
    weights = jnp.exp(logit_scores - row_max)
    probabilities = weights / jnp.sum(weights, axis=-1, keepdims=True)
    reduced_probabilities = probabilities.astype(jnp.bfloat16)
    attention_result = jnp.einsum(
        "htk,hkd->htd", reduced_probabilities, value_all, preferred_element_type=jnp.float32
    ).astype(jnp.bfloat16)
    partial_out = jnp.einsum(
        "htd,hde->te", attention_result, out_weight, preferred_element_type=jnp.float32
    )
    summed = lax.psum(partial_out.astype(jnp.bfloat16), "head").astype(jnp.float32)
    columns = summed.shape[1] // lax.axis_size("head")
    result = lax.dynamic_slice_in_dim(summed, lax.axis_index("head") * columns, columns, 1)
    projected = result.astype(jnp.bfloat16)
    full_grad = lax.all_gather(out_cotangent, "head", axis=1, tiled=True)
    grad_att = jnp.einsum(
        "te,hde->htd", full_grad, out_weight, preferred_element_type=jnp.float32
    ).astype(jnp.bfloat16)
    row_delta = jnp.sum(
        grad_att.astype(jnp.float32) * attention_result.astype(jnp.float32), axis=-1, keepdims=True
    )
    probability_gradient = jnp.einsum(
        "htd,hkd->htk", grad_att, value_all, preferred_element_type=jnp.float32
    )
    score_gradient = (probabilities * (probability_gradient - row_delta) * score_scale).astype(
        jnp.bfloat16
    )
    gradient_of_queries = jnp.einsum(
        "htk,hkd->htd", score_gradient, key_all, preferred_element_type=jnp.float32
    ).astype(jnp.bfloat16)
    key_part = jnp.einsum(
        "htk,htd->hkd", score_gradient, queries, preferred_element_type=jnp.float32
    )
    value_part = jnp.einsum(
        "htk,htd->hkd", reduced_probabilities, grad_att, preferred_element_type=jnp.float32
    )
    gradients = jnp.stack([key_part, value_part])
    block_rows = 2 * tok_rows
    local_grad = gradients[:, :, :block_rows].reshape(2, group_heads, 2, tok_rows, head_width)
    own_grad = jnp.where(parity == 0, local_grad[:, :, 0], local_grad[:, :, 1])
    other_grad = jnp.where(parity == 0, local_grad[:, :, 1], local_grad[:, :, 0]).astype(
        jnp.bfloat16
    )
    partner_grad = gradients[:, :, block_rows:].reshape(2, group_heads, 2, tok_rows, head_width)
    partner_grad = partner_grad.astype(jnp.bfloat16)
    returned = lax.all_to_all(
        partner_grad.reshape(2, group_heads, slot_count, devices, portion),
        "seq",
        split_axis=3,
        concat_axis=3,
        tiled=True,
    )
    summed_back = jnp.einsum(
        "hsij,chsil->chjl", select, returned, preferred_element_type=jnp.float32
    ).astype(jnp.bfloat16)
    arrived = lax.all_to_all(summed_back, "seq", split_axis=2, concat_axis=2, tiled=True)
    arrived = arrived.reshape(2, group_heads, tok_rows, head_width).astype(jnp.float32)
    pair_back = partner(other_grad, "seq", 0).astype(jnp.float32)
    total_grad = own_grad + arrived + pair_back
    key_grad = total_grad[0].astype(jnp.bfloat16)
    value_grad = total_grad[1].astype(jnp.bfloat16)
    return (projected, gradient_of_queries, key_grad, value_grad)


def per_device(*arrays):
    chips = lax.axis_size("seq") // 2
    square = chips == arrays[0].shape[0] == lax.axis_size("head") == 4
    return (by_heads if square else by_routing)(*arrays)


def solution(mesh):
    return jax.shard_map(
        per_device,
        mesh=mesh,
        in_specs=(
            P("head", "seq", None),
            P("head", "seq", None),
            P("head", "seq", None),
            P("head", None),
            P("head", None, None),
            P("seq", "head"),
        ),
        out_specs=(
            P("seq", "head"),
            P("head", "seq", None),
            P("head", "seq", None),
            P("head", "seq", None),
        ),
        check_vma=False,
    )
```
